128 devices in a mesh: lat: 4 (over z), ord: 32 (over y, x, core).
Axes of the slice: x: 4, y: 4, z: 4, core: 2. Of those that a mesh axis runs over, the one named last changes fastest.
Arguments:
- ground_field: bfloat16 [32, 2, 2048, 4096], P(None, None, ('lat', 'ord')), may hold values from -6 to 6
- legendre: bfloat16 [512, 2048, 512], P('ord', 'lat'), may hold values from -6 to 6
- quad_weights: float32 [2048], P(('lat', 'ord')), may hold values from 0.25 to 2.5
- slot_orders: int32 [512], replicated, may hold values from 0 to 511, as said below
- q_response: float32 [32, 2, 512], replicated, may hold values from -6 to 6
Outputs:
- induced_field: bfloat16 [32, 2, 2048, 4096], P(None, None, ('lat', 'ord'))
The draws below stay inside these ranges and needn't reach their ends.
Inputs may be any that keep to these rules, and one draw needn't show every extreme that they name: slot_orders is a permutation of 0 to 511, and slots 2q and 2q + 1 hold values that sum to 511, so that every 16 consecutive slots carry the same number of degrees at or above their orders.
All inputs are finite; a program needn't handle non-finite values.
Results may differ from the reference program's by a relative error of at most 0.008.
Values may be sent and summed in bfloat16 or wider, within the bound.
No kernel may reach another device: no remote copies, remote signals or barrier semaphores. Data moves between devices by JAX's collectives and lax.ppermute only.
A program may use at most 128 MiB of HBM per device.

```python
import math
import jax
import jax.numpy as jnp
from jax import lax

NLAT = 2048
NLON = 4096
M = 512
LMAX = 2047
F = 32


def draw_slot_orders(key, part):
    key = jax.random.fold_in(key, 7)
    first_key, second_key = jax.random.split(key)
    pairs = jax.random.permutation(first_key, M // 2).astype(jnp.int32)
    flips = jax.random.randint(second_key, (M // 2,), 0, 2).astype(jnp.int32)
    leading = jnp.where(flips == 1, M - 1 - pairs, pairs)
    trailing = M - 1 - leading
    return jnp.stack([leading, trailing], axis=1).reshape(M).astype(jnp.int32)


def block_levels(key, dims, shards, smallest, high):
    level, own = 1.0, jax.random.fold_in(key, 6)
    for dim, shards_of in shards:
        heights = jnp.exp(jax.random.uniform(jax.random.fold_in(own, dim), (shards_of,), jnp.float32, smallest / len(shards), high / len(shards)))
        level = level * jnp.repeat(heights, dims[dim] // shards_of).reshape([-1 if axis == dim else 1 for axis in range(len(dims))])
    return level


def noise(stream_key, extent, scale, reach, cuts=(), kind=jnp.bfloat16):
    drawn = scale * jax.random.normal(stream_key, extent, jnp.float32)
    if cuts:
        drawn = drawn * block_levels(stream_key, extent, cuts, -0.22, 0.18)
    return jnp.clip(drawn, -reach, reach).astype(kind)


def setup_inputs(seed: int = 0) -> dict:
    seeds = jax.random.split(jax.random.key(seed), 6)
    ground_field = noise(seeds[0], (F, 2, NLAT, NLON), 1.0, 6.0, ((2, 128),))
    legendre = noise(seeds[1], (M, NLAT, M), 1.0, 6.0, ((0, 32), (1, 4)))
    quad_weights = jnp.clip(jnp.exp(math.log(2.5) - 2.3025851 * jax.random.uniform(seeds[2], (NLAT,), jnp.float32) ** block_levels(seeds[2], (NLAT,), ((0, 128),), -0.2, 0.2)), 0.25, 2.5)
    slot_orders = draw_slot_orders(jax.random.fold_in(seeds[5], 71), 0)
    q_response = noise(seeds[4], (F, 2, M), 1.0, 6.0, (), jnp.float32)
    return {"ground_field": ground_field, "legendre": legendre, "quad_weights": quad_weights, "slot_orders": slot_orders, "q_response": q_response}


def fourier_table(slot_orders):
    orders = LMAX + 1 - M + slot_orders.astype(jnp.int32)
    longitudes = jnp.arange(NLON, dtype=jnp.int32)
    phase_index = longitudes[:, None] * orders[None, :] % NLON
    angles = phase_index.astype(jnp.float32) * (2.0 * math.pi / NLON)
    return jnp.concatenate([jnp.cos(angles), -jnp.sin(angles)], axis=1).astype(jnp.bfloat16)

def reference(ground_field, legendre, quad_weights, slot_orders, q_response):
    fourier_basis = fourier_table(slot_orders)
    factor = quad_weights / math.sqrt(NLON)

    def forward(slice_block):
        transformed = jnp.dot(slice_block.reshape(2 * NLAT, NLON), fourier_basis, preferred_element_type=jnp.float32)
        scaled = transformed.reshape(2, NLAT, 2, M) * factor[None, :, None, None]
        return scaled.astype(jnp.bfloat16)
    spectra = lax.map(forward, ground_field)
    by_slot = jnp.moveaxis(spectra, 4, 0)

    def analyse(operands):
        spec_slot, legendre_slot = operands
        stacked = jnp.transpose(spec_slot, (0, 1, 3, 2)).reshape(4 * F, NLAT)
        summed = jnp.dot(stacked, legendre_slot, preferred_element_type=jnp.float32)
        return (summed * (1.0 / math.sqrt(NLAT))).reshape(F, 2, 2, M)
    coefficients = lax.map(analyse, (by_slot, legendre))
    q_real = q_response[:, 0, :][None, :, None, :]
    q_imag = q_response[:, 1, :][None, :, None, :]
    field_real = coefficients[:, :, 0]
    field_imag = coefficients[:, :, 1]
    induced_real = q_real * field_real - q_imag * field_imag
    induced_imag = q_real * field_imag + q_imag * field_real
    valid_degree = jnp.arange(M, dtype=jnp.int32)[None, :] >= slot_orders.astype(jnp.int32)[:, None]
    stacked_parts = jnp.stack([induced_real, induced_imag], axis=2)
    induced_coeff = jnp.where(valid_degree[:, None, None, None, :], stacked_parts, jnp.float32(0.0)).astype(jnp.bfloat16)

    def synthesize(operands):
        coeff_slot, legendre_slot = operands
        summed = jnp.dot(coeff_slot.reshape(4 * F, M), legendre_slot.T, preferred_element_type=jnp.float32)
        return (summed * (1.0 / math.sqrt(M))).astype(jnp.bfloat16).reshape(F, 2, 2, NLAT)
    synthesized = lax.map(synthesize, (induced_coeff, legendre))

    def inverse(slice_block):
        stacked = jnp.transpose(slice_block, (1, 3, 2, 0)).reshape(2 * NLAT, 2 * M)
        summed = jnp.dot(stacked, fourier_basis.T, preferred_element_type=jnp.float32)
        return (summed * (1.0 / math.sqrt(2 * M))).astype(jnp.bfloat16).reshape(2, NLAT, NLON)
    return lax.map(inverse, jnp.moveaxis(synthesized, 1, 0))
```

```python
import functools
import math

import jax
import jax.numpy as jnp
from jax import lax
from jax.experimental import pallas as pl
from jax.experimental.pallas import tpu as pltpu
from jax.sharding import PartitionSpec as P

NLAT = 2048
NLON = 4096
HALF = 2048
M = 512
LMAX = 2047
F = 32
ROWS = 16
LATS = 4
OWNERS = 32
PAIRS = 8
COLS = 256
WIDE = 128
PARTS = 4 * PAIRS + 1
MIB = 1 << 20


def cos_sin(phase):
    quadrant = (phase + 512) >> 10
    x = (phase - (quadrant << 10)).astype(jnp.float32) * (2.0 * math.pi / NLON)
    y = x * x
    c = 1.0 + y * (-0.5 + y * (1.0 / 24 + y * (-1.0 / 720 + y * (1.0 / 40320))))
    s = x * (1.0 + y * (-1.0 / 6 + y * (1.0 / 120 + y * (-1.0 / 5040 + y * (1.0 / 362880)))))
    swap = (quadrant & 1) == 1
    cos = jnp.where(swap, s, c)
    sin = jnp.where(swap, c, s)
    cos = jnp.where(((quadrant + 1) & 2) == 2, -cos, cos)
    sin = jnp.where((quadrant & 2) == 2, -sin, sin)
    return cos, sin


def table_kernel(order_ref, out_ref):
    for parity in range(2):
        even = order_ref[...]
        order = LMAX + 1 - M + (even if parity == 0 else M - 1 - even)
        low = lax.broadcasted_iota(jnp.int32, (128, COLS), 0)
        cb, sb = cos_sin((low * order) & (NLON - 1))
        high = lax.broadcasted_iota(jnp.int32, (16, COLS), 0)
        ca, sa = cos_sin((high * 128 * order) & (NLON - 1))
        for a in range(16):
            c1, s1 = ca[a : a + 1], sa[a : a + 1]
            rows = slice(a * 128, (a + 1) * 128)
            out_ref[parity, rows, :COLS] = (c1 * cb - s1 * sb).astype(jnp.bfloat16)
            out_ref[parity, rows, COLS:] = (-(s1 * cb + c1 * sb)).astype(jnp.bfloat16)


def turned_table_kernel(order_ref, out_ref):
    for parity in range(2):
        even = order_ref[...]
        order = LMAX + 1 - M + (even if parity == 0 else M - 1 - even)
        low = lax.broadcasted_iota(jnp.int32, (COLS, 128), 1)
        cb, sb = cos_sin((low * order) & (NLON - 1))
        high = lax.broadcasted_iota(jnp.int32, (COLS, 128), 1) & 15
        ca, sa = cos_sin((high * 128 * order) & (NLON - 1))
        for a in range(16):
            c1, s1 = ca[:, a : a + 1], sa[:, a : a + 1]
            lanes = slice(a * 128, (a + 1) * 128)
            out_ref[parity, :COLS, lanes] = (c1 * cb - s1 * sb).astype(jnp.bfloat16)
            out_ref[parity, COLS:, lanes] = (-(s1 * cb + c1 * sb)).astype(jnp.bfloat16)


def forward_kernel(weight_ref, field_ref, table_ref, out_ref, sums, turned):
    step = pl.program_id(0)
    field = field_ref[...].reshape(256, NLON)
    near, far = field[:, :HALF], field[:, HALF:]
    for parity in range(2):
        folded = near + far if parity == 0 else near - far
        product = jnp.dot(folded, table_ref[parity], preferred_element_type=jnp.float32)
        for part in range(4):
            sums[parity, part, pl.ds(pl.multiple_of(step * 256, 256), 256), :] = product[:, part * 128 : part * 128 + 128]

    @pl.when(step == pl.num_programs(0) - 1)
    def _():
        for parity in range(2):
            for block in range(2):

                @pl.loop(0, ROWS)
                def _(k):
                    factor = weight_ref[k] * (1.0 / math.sqrt(NLON))
                    pieces = {}
                    for t in range(2):
                        for c in range(2):
                            pieces[t, c] = sums[parity, 2 * t + block, pl.ds(c * ROWS + k, F, stride=2 * ROWS), :]
                    stacked = jnp.concatenate(
                        [
                            pieces[t, c][8 * high : 8 * high + 8]
                            for high in range(4)
                            for t in range(2)
                            for c in range(2)
                        ],
                        axis=0,
                    )
                    turned[pl.ds(k, 128, stride=ROWS), :] = (stacked * factor).T

                out_ref[block * 16 : block * 16 + 16, parity] = (
                    turned[...].astype(jnp.bfloat16).reshape(16, PAIRS, ROWS, WIDE)
                )


def pair_facts(orders_ref, meta_ref, p):
    first = orders_ref[(meta_ref[1] * PAIRS + p) * 2]
    high_slot = jnp.where(first >= M // 2, 0, 1)
    lower = jnp.minimum(first, M - 1 - first)
    high_parity = (M - 1 - lower) & 1
    return high_slot, high_parity, lower


def analysis_kernel(orders_ref, meta_ref, spec_ref, low_ref, high_ref, o0, o1, o2, o3, whole, extras):
    p = pl.program_id(0)
    _, high_parity, lower = pair_facts(orders_ref, meta_ref, p)
    low_spec = spec_ref[:, 1 - high_parity, p].reshape(M, WIDE)
    high_spec = spec_ref[:, high_parity, p].reshape(M, WIDE)
    dims = (((0,), (0,)), ((), ()))
    low = lax.dot_general(low_spec, low_ref[0], dims, preferred_element_type=jnp.float32)
    high = lax.dot_general(high_spec, high_ref[0], dims, preferred_element_type=jnp.float32)
    lane = lax.broadcasted_iota(jnp.int32, (WIDE, 256), 1)
    moved = pltpu.roll(low[:, :256], (256 - lower) & 255, 1)
    whole[:, :256] = low[:, 256:]
    whole[:, 256:] = jnp.where(lane < 255 - lower, moved, high)
    lane = lax.broadcasted_iota(jnp.int32, (WIDE, 128), 1)
    extra = pltpu.roll(low[:, 128:256], p + 1, 1)

    @pl.when(p == 0)
    def _():
        extras[...] = jnp.zeros_like(extras)

    extras[...] = jnp.where(lane == p, extra, extras[...])
    for d, out in enumerate((o0, o1, o2, o3)):
        rows = pl.ds(pl.multiple_of(((meta_ref[0] + d) & 3) * 32, 32), 32)
        for part in range(4):
            out[4 * p + part] = whole[rows, part * 128 : part * 128 + 128].astype(out.dtype)
        out[PARTS - 1] = extras[rows, :].astype(out.dtype)


def respond_kernel(orders_ref, meta_ref, q_ref, own, r1, r2, r3, out):
    block = pl.ds(pl.multiple_of(meta_ref[0] * 8, 8), 8)
    scale = 1.0 / math.sqrt(NLAT)

    def respond(part, qr, qi):
        total = own[part] + r1[part].astype(jnp.float32)
        total = total + r2[part].astype(jnp.float32) + r3[part].astype(jnp.float32)
        total = total * scale
        pieces = []
        for t in range(2):
            real, imag = total[16 * t : 16 * t + 8], total[16 * t + 8 : 16 * t + 16]
            pieces += [qr * real - qi * imag, qr * imag + qi * real]
        out[part] = jnp.concatenate(pieces, axis=0).astype(jnp.bfloat16)

    qr, qi = q_ref[0, block, :], q_ref[1, block, :]
    lane = lax.broadcasted_iota(jnp.int32, (8, 256), 1)
    for p in range(PAIRS):
        _, _, lower = pair_facts(orders_ref, meta_ref, p)
        shift = (256 - lower) & 255
        merged = [
            jnp.where(lane < 255 - lower, pltpu.roll(q[:, :256], shift, 1), q[:, 256:]) for q in (qr, qi)
        ]
        for part in range(2):
            lanes = slice(part * 128, part * 128 + 128)
            respond(4 * p + part, qr[:, 256:][:, lanes], qi[:, 256:][:, lanes])
            respond(4 * p + 2 + part, merged[0][:, lanes], merged[1][:, lanes])
    respond(
        PARTS - 1,
        jnp.broadcast_to(qr[:, 255:256], (8, 128)),
        jnp.broadcast_to(qi[:, 255:256], (8, 128)),
    )


def synthesis_kernel(orders_ref, meta_ref, c0, c1, c2, c3, low_ref, high_ref, out_ref, whole):
    p = pl.program_id(0)
    _, high_parity, lower = pair_facts(orders_ref, meta_ref, p)
    for d, coeff in enumerate((c0, c1, c2, c3)):
        rows = pl.ds(pl.multiple_of(((meta_ref[0] + d) & 3) * 32, 32), 32)
        for part in range(4):
            whole[rows, part * 128 : part * 128 + 128] = coeff[4 * p + part].astype(jnp.float32)
        whole[rows, 512:640] = coeff[PARTS - 1].astype(jnp.float32)
    lane = lax.broadcasted_iota(jnp.int32, (WIDE, 256), 1)
    merged = whole[:, 256:512]
    moved = pltpu.roll(merged, lower, 1)
    extra = pltpu.roll(whole[:, 512:640], 127 - p, 1)
    extra = jnp.concatenate([extra, extra], axis=1)
    head = jnp.where(lane == 255, extra, jnp.where(lane >= lower, moved, 0.0))
    low = jnp.concatenate([head.astype(jnp.bfloat16), whole[:, :256].astype(jnp.bfloat16)], axis=1)
    high = jnp.where(lane >= 255 - lower, merged, 0.0).astype(jnp.bfloat16)
    dims = (((1,), (1,)), ((), ()))
    scale = 1.0 / math.sqrt(M)
    low_out = lax.dot_general(low_ref[0], low, dims, preferred_element_type=jnp.float32)
    high_out = lax.dot_general(high_ref[0], high, dims, preferred_element_type=jnp.float32)
    out_ref[:, 1 - high_parity, p] = (low_out * scale).astype(jnp.bfloat16).reshape(OWNERS, ROWS, WIDE)
    out_ref[:, high_parity, p] = (high_out * scale).astype(jnp.bfloat16).reshape(OWNERS, ROWS, WIDE)


def inverse_kernel(synth_ref, table_ref, out_ref, loose, turned, left):
    @pl.when(pl.program_id(0) == 0)
    def _():
        for parity in range(2):
            loose[...] = synth_ref[:, parity].reshape(COLS * ROWS, WIDE).astype(jnp.float32)

            @pl.loop(0, ROWS)
            def _(k):
                values = loose[pl.ds(k, COLS, stride=ROWS), :].T
                for t in range(2):
                    for c in range(2):
                        at = 16 * t + 8 * c
                        rows = jnp.concatenate([values[32 * h + at : 32 * h + at + 8] for h in range(4)], axis=0)
                        for half in range(2):
                            turned[2 * t + half, pl.ds(c * ROWS + k, F, stride=2 * ROWS), :] = rows[
                                :, half * 128 : half * 128 + 128
                            ]

            for part in range(4):
                left[parity, :, part * 128 : part * 128 + 128] = turned[part].astype(jnp.bfloat16)

    rows = pl.ds(pl.multiple_of(pl.program_id(0) * 256, 256), 256)
    scale = 1.0 / math.sqrt(2 * M)
    tile = 512

    @pl.loop(0, HALF // tile)
    def _(i):
        lanes = pl.ds(pl.multiple_of(i * tile, tile), tile)
        even = jnp.dot(left[0, rows, :], table_ref[0, :, lanes], preferred_element_type=jnp.float32)
        odd = jnp.dot(left[1, rows, :], table_ref[1, :, lanes], preferred_element_type=jnp.float32)
        out_ref[:, :, lanes] = ((even + odd) * scale).astype(jnp.bfloat16).reshape(16, ROWS, tile)
        lanes = pl.ds(pl.multiple_of(HALF + i * tile, tile), tile)
        out_ref[:, :, lanes] = ((even - odd) * scale).astype(jnp.bfloat16).reshape(16, ROWS, tile)


def params(steps=0, mib=48):
    return pltpu.CompilerParams(
        dimension_semantics=("arbitrary",) * steps if steps else None, vmem_limit_bytes=mib * MIB
    )


def whole_spec(shape):
    return pl.BlockSpec(shape, lambda *_: (0,) * len(shape))


def cost(flops, size):
    return pl.CostEstimate(flops=flops, bytes_accessed=size, transcendentals=0)


def low_block(p, orders_ref, meta_ref):
    return (2 * p + 1 - pair_facts(orders_ref, meta_ref, p)[0], 0, 0)


def high_block(p, orders_ref, meta_ref):
    return (2 * p + pair_facts(orders_ref, meta_ref, p)[0], 0, 1)


LEGENDRE_SPECS = [pl.BlockSpec((1, M, M), low_block), pl.BlockSpec((1, M, M // 2), high_block)]
SMEM = pl.BlockSpec(memory_space=pltpu.SMEM)


def exchange(parts):
    return [lax.ppermute(part, "lat", [(i, (i + d) % LATS) for i in range(LATS)]) for d, part in zip((1, 2, 3), parts)]


def shards(ground_field, legendre, quad_weights, slot_orders, q_response):
    bf16, f32 = jnp.bfloat16, jnp.float32
    meta = jnp.stack([lax.axis_index("lat"), lax.axis_index("ord")]).astype(jnp.int32)
    first = slot_orders.reshape(COLS, 2)[:, 0]
    even = jnp.where((first & 1) == 0, first, M - 1 - first)

    table = pl.pallas_call(
        table_kernel,
        out_shape=jax.ShapeDtypeStruct((2, HALF, 2 * COLS), bf16),
        compiler_params=params(),
        cost_estimate=cost(1 << 26, 4 * MIB),
        name="table",
    )(even.reshape(1, COLS))

    spectra_shape = (OWNERS, 2, PAIRS, ROWS, WIDE)
    spectra = pl.pallas_call(
        forward_kernel,
        grid=(4,),
        in_specs=[
            SMEM,
            pl.BlockSpec((16, ROWS, NLON), lambda i: (i, 0, 0)),
            whole_spec((2, HALF, 2 * COLS)),
        ],
        out_specs=whole_spec(spectra_shape),
        out_shape=jax.ShapeDtypeStruct(spectra_shape, bf16),
        scratch_shapes=[pltpu.VMEM((2, 4, 1024, 128), f32), pltpu.VMEM((128 * ROWS, WIDE), f32)],
        compiler_params=params(1),
        cost_estimate=cost(4 << 30, 14 * MIB),
        name="forward",
    )(quad_weights, ground_field.reshape(2 * F, ROWS, NLON), table)

    turned_table = pl.pallas_call(
        turned_table_kernel,
        out_shape=jax.ShapeDtypeStruct((2, 2 * COLS, HALF), bf16),
        compiler_params=params(),
        cost_estimate=cost(1 << 26, 4 * MIB),
        name="turned_table",
    )(even.reshape(COLS, 1))

    spectra = lax.all_to_all(spectra, "ord", split_axis=0, concat_axis=0, tiled=True)

    part_shape = (PARTS, 32, 128)
    part_spec = whole_spec(part_shape)
    partials = pl.pallas_call(
        analysis_kernel,
        grid_spec=pltpu.PrefetchScalarGridSpec(
            num_scalar_prefetch=2,
            grid=(PAIRS,),
            in_specs=[whole_spec(spectra_shape)] + LEGENDRE_SPECS,
            out_specs=[part_spec] * 4,
            scratch_shapes=[pltpu.VMEM((WIDE, M), f32), pltpu.VMEM((WIDE, 128), f32)],
        ),
        out_shape=[jax.ShapeDtypeStruct(part_shape, f32)] + [jax.ShapeDtypeStruct(part_shape, bf16)] * 3,
        compiler_params=params(1),
        cost_estimate=cost(1 << 30, 9 * MIB),
        name="analysis",
    )(slot_orders, meta, spectra, legendre, legendre)

    arrived = exchange(partials[1:])
    induced = pl.pallas_call(
        respond_kernel,
        in_specs=[SMEM, SMEM] + [pl.BlockSpec(memory_space=pltpu.VMEM)] * 5,
        out_specs=pl.BlockSpec(memory_space=pltpu.VMEM),
        out_shape=jax.ShapeDtypeStruct(part_shape, bf16),
        compiler_params=params(),
        cost_estimate=cost(1 << 22, 2 * MIB),
        name="respond",
    )(slot_orders, meta, jnp.transpose(q_response, (1, 0, 2)), partials[0], *arrived)

    behind1, behind2, behind3 = exchange([induced] * 3)
    synthesized = pl.pallas_call(
        synthesis_kernel,
        grid_spec=pltpu.PrefetchScalarGridSpec(
            num_scalar_prefetch=2,
            grid=(PAIRS,),
            in_specs=[part_spec] * 4 + LEGENDRE_SPECS,
            out_specs=whole_spec(spectra_shape),
            scratch_shapes=[pltpu.VMEM((WIDE, M + 128), f32)],
        ),
        out_shape=jax.ShapeDtypeStruct(spectra_shape, bf16),
        compiler_params=params(1),
        cost_estimate=cost(1 << 30, 9 * MIB),
        name="synthesis",
    )(slot_orders, meta, induced, behind3, behind2, behind1, legendre, legendre)

    synthesized = lax.all_to_all(synthesized, "ord", split_axis=0, concat_axis=0, tiled=True)

    field = pl.pallas_call(
        inverse_kernel,
        grid=(4,),
        in_specs=[whole_spec(spectra_shape), whole_spec((2, 2 * COLS, HALF))],
        out_specs=pl.BlockSpec((16, ROWS, NLON), lambda i: (i, 0, 0)),
        out_shape=jax.ShapeDtypeStruct((2 * F, ROWS, NLON), bf16),
        scratch_shapes=[
            pltpu.VMEM((COLS * ROWS, WIDE), f32),
            pltpu.VMEM((4, 1024, 128), f32),
            pltpu.VMEM((2, 1024, 2 * COLS), bf16),
        ],
        compiler_params=params(1),
        cost_estimate=cost(4 << 30, 14 * MIB),
        name="inverse",
    )(synthesized, turned_table)
    return field.reshape(F, 2, ROWS, NLON)


def solution(mesh):
    in_specs = (
        P(None, None, ("lat", "ord"), None),
        P("ord", "lat", None),
        P(("lat", "ord")),
        P(),
        P(),
    )
    out_specs = P(None, None, ("lat", "ord"), None)
    return jax.shard_map(shards, mesh=mesh, in_specs=in_specs, out_specs=out_specs, check_vma=False)
```

```python
import functools
import math

import jax
import jax.numpy as jnp
from jax import lax
from jax.experimental import pallas as pl
from jax.experimental.pallas import tpu as pltpu
from jax.sharding import PartitionSpec as P

NLAT = 2048
NLON = 4096
HALF = 2048
M = 512
LMAX = 2047
F = 32
ROWS = 16
LATS = 4
OWNERS = 32
PAIRS = 8
CHUNKS = 2
GROUP = PAIRS // CHUNKS
COLS = OWNERS * PAIRS
WIDE = 128
PARTS = 4 * GROUP + 1
MIB = 1 << 20


def cos_sin(phase):
    quadrant = (phase + 512) >> 10
    x = (phase - (quadrant << 10)).astype(jnp.float32) * (2.0 * math.pi / NLON)
    y = x * x
    c = 1.0 + y * (-0.5 + y * (1.0 / 24 + y * (-1.0 / 720 + y * (1.0 / 40320))))
    s = x * (1.0 + y * (-1.0 / 6 + y * (1.0 / 120 + y * (-1.0 / 5040 + y * (1.0 / 362880)))))
    swap = (quadrant & 1) == 1
    cos = jnp.where(swap, s, c)
    sin = jnp.where(swap, c, s)
    cos = jnp.where(((quadrant + 1) & 2) == 2, -cos, cos)
    sin = jnp.where((quadrant & 2) == 2, -sin, sin)
    return cos, sin


def slot_order(even, parity):
    return LMAX + 1 - M + (even if parity == 0 else M - 1 - even)


def turned_table_kernel(even_ref, out_ref):
    for parity in range(2):
        order = slot_order(even_ref[...], parity)
        low = lax.broadcasted_iota(jnp.int32, (COLS, 128), 1)
        cb, sb = cos_sin((low * order) & (NLON - 1))
        high = lax.broadcasted_iota(jnp.int32, (COLS, 128), 1) & 15
        ca, sa = cos_sin((high * 128 * order) & (NLON - 1))
        for a in range(16):
            c1, s1 = ca[:, a : a + 1], sa[:, a : a + 1]
            lanes = slice(a * 128, (a + 1) * 128)
            out_ref[parity, :COLS, lanes] = (c1 * cb - s1 * sb).astype(jnp.bfloat16)
            out_ref[parity, COLS:, lanes] = (-(s1 * cb + c1 * sb)).astype(jnp.bfloat16)


def forward_kernel(
    weight_ref, even_ref, field_ref, out_ref, fields, folded, tables, short, sums, turned, packed, field_sems, out_sems
):
    arrivals = [
        pltpu.make_async_copy(field_ref.at[pl.ds(16 * i, 16)], fields.at[pl.ds(16 * i, 16)], field_sems.at[i])
        for i in range(4)
    ]
    for copy in arrivals:
        copy.start()

    for parity in range(2):
        order = slot_order(even_ref[...], parity)
        low = lax.broadcasted_iota(jnp.int32, (128, COLS), 0)
        short[0], short[1] = cos_sin((low * order) & (NLON - 1))
        high = lax.broadcasted_iota(jnp.int32, (16, COLS), 0)
        short[2, :16], short[3, :16] = cos_sin((high * 128 * order) & (NLON - 1))

        for block in range(2):
            cols = slice(128 * block, 128 * block + 128)
            for step in range(4):
                cb, sb = short[0, :, cols], short[1, :, cols]
                for i in range(4):
                    a = step * 4 + i
                    c1, s1 = short[2, a : a + 1, cols], short[3, a : a + 1, cols]
                    at = slice(a * 128, a * 128 + 128)
                    tables[parity, block, at, :128] = (c1 * cb - s1 * sb).astype(jnp.bfloat16)
                    tables[parity, block, at, 128:] = (-(s1 * cb + c1 * sb)).astype(jnp.bfloat16)

    def multiply(parity, block, i):
        rows = slice(256 * i, 256 * i + 256)
        product = jnp.dot(folded[parity, rows, :], tables[parity, block], preferred_element_type=jnp.float32)
        for t in range(2):
            sums[block, parity, t, rows, :] = product[:, t * 128 : t * 128 + 128]

    def turn(parity, block, k):
        factor = weight_ref[k] * (1.0 / math.sqrt(NLON))
        pieces = {}
        for t in range(2):
            for c in range(2):
                pieces[t, c] = sums[block, parity, t, pl.ds(c * ROWS + k, F, stride=2 * ROWS), :]
        stacked = jnp.concatenate(
            [pieces[t, c][8 * high : 8 * high + 8] for high in range(4) for t in range(2) for c in range(2)], axis=0
        )
        turned[block, parity, pl.ds(k, 128, stride=ROWS), :] = (stacked * factor).T

    leaving = []

    def finish(parity, block):
        packed[block, parity] = turned[block, parity].astype(jnp.bfloat16).reshape(16, PAIRS, ROWS, WIDE)
        leaving.append(
            pltpu.make_async_copy(
                packed.at[block, parity], out_ref.at[pl.ds(16 * block, 16), parity], out_sems.at[block, parity]
            )
        )
        leaving[-1].start()

    for i in range(4):
        rows = slice(256 * i, 256 * i + 256)
        arrivals[i].wait()
        field = fields[16 * i : 16 * i + 16].reshape(256, NLON)
        near, far = field[:, :HALF], field[:, HALF:]
        folded[0, rows, :] = near + far
        folded[1, rows, :] = near - far
        multiply(0, 0, i)

    before = (0, 0)
    for block, parity in ((0, 1), (1, 0), (1, 1)):
        for i in range(4):
            multiply(parity, block, i)
            for k in range(4):
                turn(before[1], before[0], i * 4 + k)
        finish(before[1], before[0])
        before = (block, parity)
    for k in range(16):
        turn(1, 1, k)
    finish(1, 1)
    for copy in leaving:
        copy.wait()


def pair_facts(orders_ref, meta_ref, pair):
    first = orders_ref[(meta_ref[1] * PAIRS + pair) * 2]
    high_slot = jnp.where(first >= M // 2, 0, 1)
    lower = jnp.minimum(first, M - 1 - first)
    high_parity = (M - 1 - lower) & 1
    return high_slot, high_parity, lower


def gather_kernel(orders_ref, meta_ref, legendre_ref, _, low_ref, high_ref, sems):
    copies = []
    for p in range(PAIRS):
        high_slot, _, _ = pair_facts(orders_ref, meta_ref, p)
        copies.append(pltpu.make_async_copy(legendre_ref.at[2 * p + 1 - high_slot], low_ref.at[p], sems.at[0, p]))
        copies.append(
            pltpu.make_async_copy(
                legendre_ref.at[2 * p + high_slot, :, pl.ds(M // 2, M // 2)], high_ref.at[p], sems.at[1, p]
            )
        )
    for copy in copies:
        copy.start()
    for copy in copies:
        copy.wait()


def analysis_kernel(chunk, orders_ref, meta_ref, spec_ref, low_ref, high_ref, *refs):
    outs, (spec, whole, sems) = refs[:4], refs[4:]
    copies = [
        pltpu.make_async_copy(spec_ref.at[:, :, chunk * GROUP + p], spec.at[p], sems.at[p]) for p in range(GROUP)
    ]
    for copy in copies:
        copy.start()
    dims = (((0,), (0,)), ((), ()))
    lane = lax.broadcasted_iota(jnp.int32, (WIDE, 256), 1)
    lane1 = lax.broadcasted_iota(jnp.int32, (WIDE, 128), 1)
    extras = jnp.zeros((WIDE, 128), jnp.float32)
    for p in range(GROUP):
        pair = chunk * GROUP + p
        _, high_parity, lower = pair_facts(orders_ref, meta_ref, pair)
        copies[p].wait()
        low_spec = spec[p, :, 1 - high_parity].reshape(M, WIDE)
        high_spec = spec[p, :, high_parity].reshape(M, WIDE)
        low = lax.dot_general(low_spec, low_ref[pair], dims, preferred_element_type=jnp.float32)
        high = lax.dot_general(high_spec, high_ref[pair], dims, preferred_element_type=jnp.float32)
        moved = pltpu.roll(low[:, :256], (256 - lower) & 255, 1)
        whole[p, :, :256] = low[:, 256:]
        whole[p, :, 256:512] = jnp.where(lane < 255 - lower, moved, high)
        extras = jnp.where(lane1 == p, pltpu.roll(low[:, 128:256], p + 1, 1), extras)
        if p == GROUP - 1:
            whole[p, :, 512:] = extras
        for d, out in enumerate(outs):
            rows = pl.ds(pl.multiple_of(((meta_ref[0] + d) & 3) * 32, 32), 32)
            for part in range(5 if p == GROUP - 1 else 4):
                out[4 * p + part] = whole[p, rows, part * 128 : part * 128 + 128].astype(out.dtype)


def respond_kernel(chunk, orders_ref, meta_ref, q_ref, own, r1, r2, r3, out):
    block = pl.ds(pl.multiple_of(meta_ref[0] * 8, 8), 8)
    scale = 1.0 / math.sqrt(NLAT)

    def respond(part, qr, qi):
        total = own[part] + r1[part].astype(jnp.float32)
        total = total + r2[part].astype(jnp.float32) + r3[part].astype(jnp.float32)
        total = total * scale
        pieces = []
        for t in range(2):
            real, imag = total[16 * t : 16 * t + 8], total[16 * t + 8 : 16 * t + 16]
            pieces += [qr * real - qi * imag, qr * imag + qi * real]
        out[part] = jnp.concatenate(pieces, axis=0).astype(jnp.bfloat16)

    qr, qi = q_ref[0, block, :], q_ref[1, block, :]
    lane = lax.broadcasted_iota(jnp.int32, (8, 256), 1)
    for p in range(GROUP):
        _, _, lower = pair_facts(orders_ref, meta_ref, chunk * GROUP + p)
        shift = (256 - lower) & 255
        merged = [
            jnp.where(lane < 255 - lower, pltpu.roll(q[:, :256], shift, 1), q[:, 256:]) for q in (qr, qi)
        ]
        for part in range(2):
            lanes = slice(part * 128, part * 128 + 128)
            respond(4 * p + part, qr[:, 256:][:, lanes], qi[:, 256:][:, lanes])
            respond(4 * p + 2 + part, merged[0][:, lanes], merged[1][:, lanes])
    respond(
        PARTS - 1,
        jnp.broadcast_to(qr[:, 255:256], (8, 128)),
        jnp.broadcast_to(qi[:, 255:256], (8, 128)),
    )


def synthesis_kernel(chunk, orders_ref, meta_ref, c0, c1, c2, c3, low_ref, high_ref, *refs):
    out_ref, packed, whole, sems = refs[-4:]
    dims = (((1,), (1,)), ((), ()))
    scale = 1.0 / math.sqrt(M)
    lane = lax.broadcasted_iota(jnp.int32, (WIDE, 256), 1)
    copies = []
    for p in range(GROUP):
        pair = chunk * GROUP + p
        _, high_parity, lower = pair_facts(orders_ref, meta_ref, pair)
        for d, coeff in enumerate((c0, c1, c2, c3)):
            rows = pl.ds(pl.multiple_of(((meta_ref[0] + d) & 3) * 32, 32), 32)
            for part in range(4):
                whole[p, rows, part * 128 : part * 128 + 128] = coeff[4 * p + part].astype(jnp.float32)
            if p == 0:
                whole[0, rows, 512:640] = coeff[PARTS - 1].astype(jnp.float32)
        merged = whole[p, :, 256:512]
        moved = pltpu.roll(merged, lower, 1)
        extra = pltpu.roll(whole[0, :, 512:640], 127 - p, 1)
        extra = jnp.concatenate([extra, extra], axis=1)
        head = jnp.where(lane == 255, extra, jnp.where(lane >= lower, moved, 0.0))
        low = jnp.concatenate([head.astype(jnp.bfloat16), whole[p, :, :256].astype(jnp.bfloat16)], axis=1)
        high = jnp.where(lane >= 255 - lower, merged, 0.0).astype(jnp.bfloat16)
        low_out = lax.dot_general(low_ref[pair], low, dims, preferred_element_type=jnp.float32)
        high_out = lax.dot_general(high_ref[pair], high, dims, preferred_element_type=jnp.float32)
        packed[p, :, 1 - high_parity] = (low_out * scale).astype(jnp.bfloat16).reshape(OWNERS, ROWS, WIDE)
        packed[p, :, high_parity] = (high_out * scale).astype(jnp.bfloat16).reshape(OWNERS, ROWS, WIDE)
        copies.append(pltpu.make_async_copy(packed.at[p], out_ref.at[:, :, pair], sems.at[p]))
        copies[-1].start()
    for copy in copies:
        copy.wait()


TILE = 512
BAND = 512
TILES = HALF // TILE


def inverse_kernel(
    synth_ref, table_ref, out_ref, synth, tables, loose, turned, left, evens, packed, in_sems, table_sems, out_sems
):
    arrivals = [pltpu.make_async_copy(synth_ref.at[:, p], synth.at[p], in_sems.at[p]) for p in range(2)]
    table_arrivals = []
    for i in range(TILES):
        lanes = pl.ds(i * TILE, TILE)
        table_arrivals.append(pltpu.make_async_copy(table_ref.at[:, :, lanes], tables.at[:, :, lanes], table_sems.at[i]))
    for copy in arrivals + table_arrivals:
        copy.start()

    def loosen(parity, block, k):
        values = loose[parity, block, pl.ds(k, 128, stride=ROWS), :].T * (1.0 / math.sqrt(2 * M))
        for t in range(2):
            for c in range(2):
                at = 16 * t + 8 * c
                rows = jnp.concatenate([values[32 * h + at : 32 * h + at + 8] for h in range(4)], axis=0)
                turned[parity, 2 * t + block, pl.ds(c * ROWS + k, F, stride=2 * ROWS), :] = rows

    def widen(parity):
        arrivals[parity].wait()
        for block in range(2):
            loose[parity, block] = synth[parity, 16 * block : 16 * block + 16].reshape(128 * ROWS, WIDE).astype(jnp.float32)

    def narrow(parity):
        for part in range(4):
            left[parity, :, part * 128 : part * 128 + 128] = turned[parity, part].astype(jnp.bfloat16)

    widen(0)
    for block in range(2):
        for k in range(ROWS):
            loosen(0, block, k)
    narrow(0)
    widen(1)
    for i in range(TILES):
        lanes = slice(i * TILE, i * TILE + TILE)
        table_arrivals[i].wait()
        for r in range(0, 1024, BAND):
            rows = slice(r, r + BAND)
            evens[rows, lanes] = jnp.dot(left[0, rows, :], tables[0, :, lanes], preferred_element_type=jnp.float32)
        for block in range(2):
            for k in range(4):
                loosen(1, block, i * 4 + k)
    narrow(1)
    leaving = []
    for i in range(TILES):
        slot = i % 2
        lanes = slice(i * TILE, i * TILE + TILE)
        if i >= 2:
            for copy in leaving[2 * i - 4 : 2 * i - 2]:
                copy.wait()
        for r in range(0, 1024, BAND):
            rows = slice(r, r + BAND)
            even = evens[rows, lanes]
            odd = jnp.dot(left[1, rows, :], tables[1, :, lanes], preferred_element_type=jnp.float32)
            at = slice(r // ROWS, (r + BAND) // ROWS)
            packed[slot, 0, at] = (even + odd).astype(jnp.bfloat16).reshape(BAND // ROWS, ROWS, TILE)
            packed[slot, 1, at] = (even - odd).astype(jnp.bfloat16).reshape(BAND // ROWS, ROWS, TILE)
        for side in range(2):
            copy = pltpu.make_async_copy(
                packed.at[slot, side], out_ref.at[:, :, pl.ds(side * HALF + i * TILE, TILE)], out_sems.at[slot, side]
            )
            copy.start()
            leaving.append(copy)
    for copy in leaving[-4:]:
        copy.wait()


def params(mib=56):
    return pltpu.CompilerParams(vmem_limit_bytes=mib * MIB)


def cost(flops, size):
    return pl.CostEstimate(flops=flops, bytes_accessed=size, transcendentals=0)


def in_hbm(x):
    return pltpu.with_memory_space_constraint(x, pltpu.HBM)


SMEM = pl.BlockSpec(memory_space=pltpu.SMEM)
VMEM = pl.BlockSpec(memory_space=pltpu.VMEM)
HBM = pl.BlockSpec(memory_space=pltpu.HBM)
ANY = pl.BlockSpec(memory_space=pl.ANY)
SPECTRA = (OWNERS, 2, PAIRS, ROWS, WIDE)
PART = (PARTS, 32, 128)
LOWER, UPPER = (PAIRS, M, M), (PAIRS, M, M // 2)
bf16, f32 = jnp.bfloat16, jnp.float32


def exchange(parts):
    return [lax.ppermute(part, "lat", [(i, (i + d) % LATS) for i in range(LATS)]) for d, part in zip((1, 2, 3), parts)]


def swap_owners(values):
    return lax.all_to_all(values, "ord", split_axis=0, concat_axis=0, tiled=True)


def forward(quad_weights, even, field):
    return pl.pallas_call(
        forward_kernel,
        in_specs=[SMEM, VMEM, HBM],
        out_specs=HBM,
        out_shape=pltpu.HBM(SPECTRA, bf16),
        scratch_shapes=[
            pltpu.VMEM((2 * F, ROWS, NLON), bf16),
            pltpu.VMEM((2, 1024, HALF), bf16),
            pltpu.VMEM((2, 2, HALF, 256), bf16),
            pltpu.VMEM((4, 128, COLS), f32),
            pltpu.VMEM((2, 2, 2, 1024, 128), f32),
            pltpu.VMEM((2, 2, 128 * ROWS, WIDE), f32),
            pltpu.VMEM((2, 2, 16, PAIRS, ROWS, WIDE), bf16),
            pltpu.SemaphoreType.DMA((4,)),
            pltpu.SemaphoreType.DMA((2, 2)),
        ],
        compiler_params=params(48),
        cost_estimate=cost(4 << 30, 10 * MIB),
        name="forward",
    )(quad_weights, even, in_hbm(field))


def turned_tables(even):
    return pl.pallas_call(
        turned_table_kernel,
        in_specs=[VMEM],
        out_specs=VMEM,
        out_shape=jax.ShapeDtypeStruct((2, 2 * COLS, HALF), bf16),
        compiler_params=params(16),
        cost_estimate=cost(1 << 26, 4 * MIB),
        name="turned_table",
    )(even)


def gather(slot_orders, meta, legendre, spectra):
    return pl.pallas_call(
        gather_kernel,
        in_specs=[SMEM, SMEM, HBM, ANY],
        out_specs=[VMEM, VMEM],
        out_shape=[jax.ShapeDtypeStruct(LOWER, bf16), jax.ShapeDtypeStruct(UPPER, bf16)],
        scratch_shapes=[pltpu.SemaphoreType.DMA((2, PAIRS))],
        compiler_params=params(16),
        cost_estimate=cost(1 << 20, 12 * MIB),
        name="gather",
    )(slot_orders, meta, in_hbm(legendre), spectra)


def analysis(chunk, slot_orders, meta, spectra, tables):
    return pl.pallas_call(
        functools.partial(analysis_kernel, chunk),
        in_specs=[SMEM, SMEM, ANY, VMEM, VMEM],
        out_specs=[VMEM] * 4,
        out_shape=[jax.ShapeDtypeStruct(PART, f32)] + [jax.ShapeDtypeStruct(PART, bf16)] * 3,
        scratch_shapes=[
            pltpu.VMEM((GROUP, OWNERS, 2, ROWS, WIDE), bf16),
            pltpu.VMEM((GROUP, WIDE, M + 128), f32),
            pltpu.SemaphoreType.DMA((GROUP,)),
        ],
        compiler_params=params(16),
        cost_estimate=cost(1 << 29, 4 * MIB),
        name="analysis",
    )(slot_orders, meta, spectra, *tables)


def respond(chunk, slot_orders, meta, response, own, arrived):
    return pl.pallas_call(
        functools.partial(respond_kernel, chunk),
        in_specs=[SMEM, SMEM] + [VMEM] * 5,
        out_specs=VMEM,
        out_shape=jax.ShapeDtypeStruct(PART, bf16),
        compiler_params=params(16),
        cost_estimate=cost(1 << 22, 2 * MIB),
        name="respond",
    )(slot_orders, meta, response, own, *arrived)


def synthesis(chunk, slot_orders, meta, coeffs, tables, earlier):
    return pl.pallas_call(
        functools.partial(synthesis_kernel, chunk),
        in_specs=[SMEM, SMEM] + [VMEM] * 6 + [HBM] * len(earlier),
        out_specs=HBM,
        out_shape=pltpu.HBM(SPECTRA, bf16),
        scratch_shapes=[
            pltpu.VMEM((GROUP, OWNERS, 2, ROWS, WIDE), bf16),
            pltpu.VMEM((GROUP, WIDE, M + 128), f32),
            pltpu.SemaphoreType.DMA((GROUP,)),
        ],
        input_output_aliases={8: 0} if earlier else {},
        compiler_params=params(16),
        cost_estimate=cost(1 << 29, 4 * MIB),
        name="synthesis",
    )(slot_orders, meta, *coeffs, *tables, *earlier)


def inverse(synthesized, table):
    return pl.pallas_call(
        inverse_kernel,
        in_specs=[ANY, ANY],
        out_specs=HBM,
        out_shape=pltpu.HBM((2 * F, ROWS, NLON), bf16),
        scratch_shapes=[
            pltpu.VMEM((2, OWNERS, PAIRS, ROWS, WIDE), bf16),
            pltpu.VMEM((2, 2 * COLS, HALF), bf16),
            pltpu.VMEM((2, 2, 128 * ROWS, WIDE), f32),
            pltpu.VMEM((2, 4, 1024, 128), f32),
            pltpu.VMEM((2, 1024, 2 * COLS), bf16),
            pltpu.VMEM((1024, HALF), f32),
            pltpu.VMEM((2, 2, 2 * F, ROWS, TILE), bf16),
            pltpu.SemaphoreType.DMA((2,)),
            pltpu.SemaphoreType.DMA((TILES,)),
            pltpu.SemaphoreType.DMA((2, 2)),
        ],
        compiler_params=params(48),
        cost_estimate=cost(4 << 30, 14 * MIB),
        name="inverse",
    )(synthesized, table)


def shards(ground_field, legendre, quad_weights, slot_orders, q_response):
    meta = jnp.stack([lax.axis_index("lat"), lax.axis_index("ord")]).astype(jnp.int32)
    first = slot_orders.reshape(COLS, 2)[:, 0]
    even = jnp.where((first & 1) == 0, first, M - 1 - first)
    response = jnp.transpose(q_response, (1, 0, 2))

    spectra = forward(quad_weights, even.reshape(1, COLS), ground_field.reshape(2 * F, ROWS, NLON))
    tables = gather(slot_orders, meta, legendre, spectra)
    spectra = swap_owners(spectra)
    owns, partials = [], []
    for c in range(CHUNKS):
        own, *sent = analysis(c, slot_orders, meta, spectra, tables)
        owns.append(own)
        partials.append(exchange(sent))
    coeffs = []
    for c in range(CHUNKS):
        induced = respond(c, slot_orders, meta, response, owns[c], partials[c])
        behind1, behind2, behind3 = exchange([induced] * 3)
        coeffs.append((induced, behind3, behind2, behind1))
    synthesized = []
    for c in range(CHUNKS):
        synthesized = [synthesis(c, slot_orders, meta, coeffs[c], tables, synthesized)]
    even, synthesized = lax.optimization_barrier((even, synthesized[0]))
    field = inverse(swap_owners(synthesized), turned_tables(even.reshape(COLS, 1)))
    return field.reshape(F, 2, ROWS, NLON)


def solution(mesh):
    in_specs = (
        P(None, None, ("lat", "ord"), None),
        P("ord", "lat", None),
        P(("lat", "ord")),
        P(),
        P(),
    )
    out_specs = P(None, None, ("lat", "ord"), None)
    return jax.shard_map(shards, mesh=mesh, in_specs=in_specs, out_specs=out_specs, check_vma=False)
```

```python
import functools
import math

import jax
import jax.numpy as jnp
from jax import lax
from jax.experimental import pallas as pl
from jax.experimental.pallas import tpu as pltpu
from jax.sharding import PartitionSpec as P

NLAT = 2048
NLON = 4096
HALF = 2048
M = 512
LMAX = 2047
F = 32
ROWS = 16
LATS = 4
OWNERS = 32
PAIRS = 8
CHUNKS = 2
GROUP = PAIRS // CHUNKS
COLS = OWNERS * PAIRS
WIDE = 128
PARTS = 4 * GROUP + 1
MIB = 1 << 20


def cos_sin(phase):
    quadrant = (phase + 512) >> 10
    x = (phase - (quadrant << 10)).astype(jnp.float32) * (2.0 * math.pi / NLON)
    y = x * x
    c = 1.0 + y * (-0.5 + y * (1.0 / 24 + y * (-1.0 / 720 + y * (1.0 / 40320))))
    s = x * (1.0 + y * (-1.0 / 6 + y * (1.0 / 120 + y * (-1.0 / 5040 + y * (1.0 / 362880)))))
    swap = (quadrant & 1) == 1
    cos = jnp.where(swap, s, c)
    sin = jnp.where(swap, c, s)
    cos = jnp.where(((quadrant + 1) & 2) == 2, -cos, cos)
    sin = jnp.where((quadrant & 2) == 2, -sin, sin)
    return cos, sin


def slot_order(even, parity):
    return LMAX + 1 - M + (even if parity == 0 else M - 1 - even)


def turned_table_kernel(even_ref, out_ref):
    for parity in range(2):
        order = slot_order(even_ref[...], parity)
        low = lax.broadcasted_iota(jnp.int32, (COLS, 128), 1)
        cb, sb = cos_sin((low * order) & (NLON - 1))
        high = lax.broadcasted_iota(jnp.int32, (COLS, 128), 1) & 15
        ca, sa = cos_sin((high * 128 * order) & (NLON - 1))
        for a in range(16):
            c1, s1 = ca[:, a : a + 1], sa[:, a : a + 1]
            lanes = slice(a * 128, (a + 1) * 128)
            out_ref[parity, :COLS, lanes] = (c1 * cb - s1 * sb).astype(jnp.bfloat16)
            out_ref[parity, COLS:, lanes] = (-(s1 * cb + c1 * sb)).astype(jnp.bfloat16)


def forward_kernel(
    weight_ref, even_ref, field_ref, out_ref, fields, folded, tables, sums, turned, packed, weights, field_sems, out_sems, weight_sem
):
    arrivals = [
        pltpu.make_async_copy(field_ref.at[pl.ds(16 * i, 16)], fields.at[pl.ds(16 * i, 16)], field_sems.at[i])
        for i in range(4)
    ]
    weight_copy = pltpu.make_async_copy(weight_ref, weights, weight_sem.at[0])
    for copy in arrivals + [weight_copy]:
        copy.start()

    def fill(parity, block):
        cols = slice(128 * block, 128 * block + 128)
        order = slot_order(even_ref[:, cols], parity)
        low = lax.broadcasted_iota(jnp.int32, (128, 128), 0)
        cb, sb = cos_sin((low * order) & (NLON - 1))
        high = lax.broadcasted_iota(jnp.int32, (16, 128), 0)
        ca, sa = cos_sin((high * 128 * order) & (NLON - 1))
        for a in range(16):
            c1, s1 = ca[a : a + 1], sa[a : a + 1]
            at = slice(a * 128, a * 128 + 128)
            tables[parity, block, at, :128] = (c1 * cb - s1 * sb).astype(jnp.bfloat16)
            tables[parity, block, at, 128:] = (-(s1 * cb + c1 * sb)).astype(jnp.bfloat16)

    for block in range(2):
        for parity in range(2):
            fill(parity, block)

    def multiply(parity, block, i):
        rows = slice(256 * i, 256 * i + 256)
        product = jnp.dot(folded[parity, rows, :], tables[parity, block], preferred_element_type=jnp.float32)
        for t in range(2):
            sums[block, parity, t, rows, :] = product[:, t * 128 : t * 128 + 128]

    def turn(parity, block, k):
        factor = weights[k] * (1.0 / math.sqrt(NLON))
        pieces = {}
        for t in range(2):
            for c in range(2):
                pieces[t, c] = sums[block, parity, t, pl.ds(c * ROWS + k, F, stride=2 * ROWS), :]
        stacked = jnp.concatenate(
            [pieces[t, c][8 * high : 8 * high + 8] for high in range(4) for t in range(2) for c in range(2)], axis=0
        )
        turned[block, parity, pl.ds(k, 128, stride=ROWS), :] = (stacked * factor).T

    leaving = []

    def finish(parity, block):
        packed[block, parity] = turned[block, parity].astype(jnp.bfloat16).reshape(16, PAIRS, ROWS, WIDE)
        leaving.append(
            pltpu.make_async_copy(
                packed.at[block, parity], out_ref.at[pl.ds(16 * block, 16), parity], out_sems.at[block, parity]
            )
        )
        leaving[-1].start()

    for i in range(4):
        rows = slice(256 * i, 256 * i + 256)
        arrivals[i].wait()
        field = fields[16 * i : 16 * i + 16].reshape(256, NLON)
        near, far = field[:, :HALF], field[:, HALF:]
        folded[0, rows, :] = near + far
        folded[1, rows, :] = near - far
        multiply(0, 0, i)

    weight_copy.wait()
    before = (0, 0)
    for block, parity in ((0, 1), (1, 0), (1, 1)):
        for i in range(4):
            multiply(parity, block, i)
            for k in range(4):
                turn(before[1], before[0], i * 4 + k)
        finish(before[1], before[0])
        before = (block, parity)
    for k in range(16):
        turn(1, 1, k)
    finish(1, 1)
    for copy in leaving:
        copy.wait()


def pair_facts(orders_ref, meta_ref, pair):
    first = orders_ref[(meta_ref[1] * PAIRS + pair) * 2]
    high_slot = jnp.where(first >= M // 2, 0, 1)
    lower = jnp.minimum(first, M - 1 - first)
    high_parity = (M - 1 - lower) & 1
    return high_slot, high_parity, lower


def legendre_copies(orders_ref, meta_ref, legendre_ref, tables, sems):
    copies = []
    for p in range(PAIRS):
        high_slot, _, _ = pair_facts(orders_ref, meta_ref, p)
        low, high = tables[2 * (p // GROUP)].at[p % GROUP], tables[2 * (p // GROUP) + 1].at[p % GROUP]
        copies.append(
            (
                pltpu.make_async_copy(legendre_ref.at[2 * p + 1 - high_slot], low, sems.at[0, p]),
                pltpu.make_async_copy(legendre_ref.at[2 * p + high_slot, :, pl.ds(M // 2, M // 2)], high, sems.at[1, p]),
            )
        )
    return copies


def first_analysis_kernel(orders_ref, meta_ref, spec_ref, legendre_ref, *refs):
    outs, tables, (whole, sems) = refs[:4], refs[4:8], refs[8:]
    copies = legendre_copies(orders_ref, meta_ref, legendre_ref, tables, sems)
    for pair in copies:
        for copy in pair:
            copy.start()
    analyse(0, orders_ref, meta_ref, spec_ref, tables[0], tables[1], outs, whole, copies)
    for pair in copies[GROUP:]:
        for copy in pair:
            copy.wait()


def second_analysis_kernel(orders_ref, meta_ref, spec_ref, low_ref, high_ref, *refs):
    analyse(1, orders_ref, meta_ref, spec_ref, low_ref, high_ref, refs[:4], refs[4], ())


def analyse(chunk, orders_ref, meta_ref, spec_ref, low_ref, high_ref, outs, whole, copies):
    dims = (((0,), (0,)), ((), ()))
    lane = lax.broadcasted_iota(jnp.int32, (WIDE, 256), 1)
    lane1 = lax.broadcasted_iota(jnp.int32, (WIDE, 128), 1)
    extras = jnp.zeros((WIDE, 128), jnp.float32)
    for p in range(GROUP):
        pair = chunk * GROUP + p
        _, high_parity, lower = pair_facts(orders_ref, meta_ref, pair)
        for copy in copies[p] if copies else ():
            copy.wait()
        low_spec = spec_ref[:, 1 - high_parity, pair].reshape(M, WIDE)
        high_spec = spec_ref[:, high_parity, pair].reshape(M, WIDE)
        low = lax.dot_general(low_spec, low_ref[p], dims, preferred_element_type=jnp.float32)
        high = lax.dot_general(high_spec, high_ref[p], dims, preferred_element_type=jnp.float32)
        moved = pltpu.roll(low[:, :256], (256 - lower) & 255, 1)
        whole[p, :, :256] = low[:, 256:]
        whole[p, :, 256:512] = jnp.where(lane < 255 - lower, moved, high)
        extras = jnp.where(lane1 == p, pltpu.roll(low[:, 128:256], p + 1, 1), extras)
        if p == GROUP - 1:
            whole[p, :, 512:] = extras
        for d, out in enumerate(outs):
            rows = pl.ds(pl.multiple_of(((meta_ref[0] + d) & 3) * 32, 32), 32)
            for part in range(5 if p == GROUP - 1 else 4):
                out[4 * p + part] = whole[p, rows, part * 128 : part * 128 + 128].astype(out.dtype)


def respond_kernel(chunk, orders_ref, meta_ref, q_ref, own, r1, r2, r3, out):
    block = pl.ds(pl.multiple_of(meta_ref[0] * 8, 8), 8)
    scale = 1.0 / math.sqrt(NLAT)

    def respond(part, qr, qi):
        total = own[part] + r1[part].astype(jnp.float32)
        total = total + r2[part].astype(jnp.float32) + r3[part].astype(jnp.float32)
        total = total * scale
        pieces = []
        for t in range(2):
            real, imag = total[16 * t : 16 * t + 8], total[16 * t + 8 : 16 * t + 16]
            pieces += [qr * real - qi * imag, qr * imag + qi * real]
        out[part] = jnp.concatenate(pieces, axis=0).astype(jnp.bfloat16)

    qr, qi = q_ref[0, block, :], q_ref[1, block, :]
    lane = lax.broadcasted_iota(jnp.int32, (8, 256), 1)
    for p in range(GROUP):
        _, _, lower = pair_facts(orders_ref, meta_ref, chunk * GROUP + p)
        shift = (256 - lower) & 255
        merged = [
            jnp.where(lane < 255 - lower, pltpu.roll(q[:, :256], shift, 1), q[:, 256:]) for q in (qr, qi)
        ]
        for part in range(2):
            lanes = slice(part * 128, part * 128 + 128)
            respond(4 * p + part, qr[:, 256:][:, lanes], qi[:, 256:][:, lanes])
            respond(4 * p + 2 + part, merged[0][:, lanes], merged[1][:, lanes])
    respond(
        PARTS - 1,
        jnp.broadcast_to(qr[:, 255:256], (8, 128)),
        jnp.broadcast_to(qi[:, 255:256], (8, 128)),
    )


def synthesis_kernel(chunk, orders_ref, meta_ref, c0, c1, c2, c3, low_ref, high_ref, *refs):
    out_ref, packed, whole, sems = refs[-4:]
    dims = (((1,), (1,)), ((), ()))
    scale = 1.0 / math.sqrt(M)
    lane = lax.broadcasted_iota(jnp.int32, (WIDE, 256), 1)
    copies = []
    for p in range(GROUP):
        pair = chunk * GROUP + p
        _, high_parity, lower = pair_facts(orders_ref, meta_ref, pair)
        for d, coeff in enumerate((c0, c1, c2, c3)):
            rows = pl.ds(pl.multiple_of(((meta_ref[0] + d) & 3) * 32, 32), 32)
            for part in range(4):
                whole[p, rows, part * 128 : part * 128 + 128] = coeff[4 * p + part].astype(jnp.float32)
            if p == 0:
                whole[0, rows, 512:640] = coeff[PARTS - 1].astype(jnp.float32)
        merged = whole[p, :, 256:512]
        moved = pltpu.roll(merged, lower, 1)
        extra = pltpu.roll(whole[0, :, 512:640], 127 - p, 1)
        extra = jnp.concatenate([extra, extra], axis=1)
        head = jnp.where(lane == 255, extra, jnp.where(lane >= lower, moved, 0.0))
        low = jnp.concatenate([head.astype(jnp.bfloat16), whole[p, :, :256].astype(jnp.bfloat16)], axis=1)
        high = jnp.where(lane >= 255 - lower, merged, 0.0).astype(jnp.bfloat16)
        low_out = lax.dot_general(low_ref[p], low, dims, preferred_element_type=jnp.float32)
        high_out = lax.dot_general(high_ref[p], high, dims, preferred_element_type=jnp.float32)
        packed[p, :, 1 - high_parity] = (low_out * scale).astype(jnp.bfloat16).reshape(OWNERS, ROWS, WIDE)
        packed[p, :, high_parity] = (high_out * scale).astype(jnp.bfloat16).reshape(OWNERS, ROWS, WIDE)
        copies.append(pltpu.make_async_copy(packed.at[p], out_ref.at[:, :, pair], sems.at[p]))
        copies[-1].start()
    for copy in copies:
        copy.wait()


TILE = 512
BAND = 512
TILES = HALF // TILE


def inverse_kernel(
    synth_ref, table_ref, out_ref, tables, loose, turned, left, evens, packed, table_sems, out_sems
):
    arrivals = []
    for i in range(TILES):
        lanes = pl.ds(i * TILE, TILE)
        arrivals.append(pltpu.make_async_copy(table_ref.at[:, :, lanes], tables.at[:, :, lanes], table_sems.at[i]))
        arrivals[i].start()

    def loosen(parity, block, k):
        values = loose[parity, block, pl.ds(k, 128, stride=ROWS), :].T * (1.0 / math.sqrt(2 * M))
        for t in range(2):
            for c in range(2):
                at = 16 * t + 8 * c
                rows = jnp.concatenate([values[32 * h + at : 32 * h + at + 8] for h in range(4)], axis=0)
                turned[parity, 2 * t + block, pl.ds(c * ROWS + k, F, stride=2 * ROWS), :] = rows

    def widen(parity):
        for block in range(2):
            loose[parity, block] = synth_ref[16 * block : 16 * block + 16, parity].reshape(128 * ROWS, WIDE).astype(jnp.float32)

    def narrow(parity):
        for part in range(4):
            left[parity, :, part * 128 : part * 128 + 128] = turned[parity, part].astype(jnp.bfloat16)

    widen(0)
    for block in range(2):
        for k in range(ROWS):
            loosen(0, block, k)
    narrow(0)
    widen(1)
    for i in range(TILES):
        lanes = slice(i * TILE, i * TILE + TILE)
        arrivals[i].wait()
        for r in range(0, 1024, BAND):
            rows = slice(r, r + BAND)
            evens[rows, lanes] = jnp.dot(left[0, rows, :], tables[0, :, lanes], preferred_element_type=jnp.float32)
        for block in range(2):
            for k in range(ROWS // TILES):
                loosen(1, block, i * (ROWS // TILES) + k)
    narrow(1)
    leaving = []
    for i in range(TILES):
        slot = i % 2
        lanes = slice(i * TILE, i * TILE + TILE)
        if i >= 2:
            for copy in leaving[2 * i - 4 : 2 * i - 2]:
                copy.wait()
        for r in range(0, 1024, BAND):
            rows = slice(r, r + BAND)
            even = evens[rows, lanes]
            odd = jnp.dot(left[1, rows, :], tables[1, :, lanes], preferred_element_type=jnp.float32)
            at = slice(r // ROWS, (r + BAND) // ROWS)
            packed[slot, 0, at] = (even + odd).astype(jnp.bfloat16).reshape(BAND // ROWS, ROWS, TILE)
            packed[slot, 1, at] = (even - odd).astype(jnp.bfloat16).reshape(BAND // ROWS, ROWS, TILE)
        for side in range(2):
            copy = pltpu.make_async_copy(
                packed.at[slot, side], out_ref.at[:, :, pl.ds(side * HALF + i * TILE, TILE)], out_sems.at[slot, side]
            )
            copy.start()
            leaving.append(copy)
    for copy in leaving[-4:]:
        copy.wait()


def params(mib=56):
    return pltpu.CompilerParams(vmem_limit_bytes=mib * MIB)


def cost(flops, size):
    return pl.CostEstimate(flops=flops, bytes_accessed=size, transcendentals=0)


def in_hbm(x):
    return pltpu.with_memory_space_constraint(x, pltpu.HBM)


def in_vmem(x):
    return pltpu.with_memory_space_constraint(x, pltpu.VMEM)


SMEM = pl.BlockSpec(memory_space=pltpu.SMEM)
VMEM = pl.BlockSpec(memory_space=pltpu.VMEM)
HBM = pl.BlockSpec(memory_space=pltpu.HBM)
ANY = pl.BlockSpec(memory_space=pl.ANY)
SPECTRA = (OWNERS, 2, PAIRS, ROWS, WIDE)
PART = (PARTS, 32, 128)
LOWER, UPPER = (GROUP, M, M), (GROUP, M, M // 2)
bf16, f32 = jnp.bfloat16, jnp.float32


def exchange(parts):
    return [lax.ppermute(part, "lat", [(i, (i + d) % LATS) for i in range(LATS)]) for d, part in zip((1, 2, 3), parts)]


def swap_owners(values):
    return lax.all_to_all(values, "ord", split_axis=0, concat_axis=0, tiled=True)


def forward(quad_weights, even, field):
    return pl.pallas_call(
        forward_kernel,
        in_specs=[HBM, VMEM, HBM],
        out_specs=HBM,
        out_shape=pltpu.HBM(SPECTRA, bf16),
        scratch_shapes=[
            pltpu.VMEM((2 * F, ROWS, NLON), bf16),
            pltpu.VMEM((2, 1024, HALF), bf16),
            pltpu.VMEM((2, 2, HALF, 256), bf16),
            pltpu.VMEM((2, 2, 2, 1024, 128), f32),
            pltpu.VMEM((2, 2, 128 * ROWS, WIDE), f32),
            pltpu.VMEM((2, 2, 16, PAIRS, ROWS, WIDE), bf16),
            pltpu.SMEM((ROWS,), f32),
            pltpu.SemaphoreType.DMA((4,)),
            pltpu.SemaphoreType.DMA((2, 2)),
            pltpu.SemaphoreType.DMA((1,)),
        ],
        compiler_params=params(40),
        cost_estimate=cost(4 << 30, 10 * MIB),
        name="forward",
    )(in_hbm(quad_weights), even, in_hbm(field))


def turned_tables(even):
    return pl.pallas_call(
        turned_table_kernel,
        in_specs=[VMEM],
        out_specs=VMEM,
        out_shape=pltpu.HBM((2, 2 * COLS, HALF), bf16),
        compiler_params=params(16),
        cost_estimate=cost(1 << 26, 4 * MIB),
        name="turned_table",
    )(even)


SENT = [jax.ShapeDtypeStruct(PART, f32)] + [jax.ShapeDtypeStruct(PART, bf16)] * 3


def first_analysis(slot_orders, meta, spectra, legendre):
    outs = pl.pallas_call(
        first_analysis_kernel,
        in_specs=[SMEM, SMEM, VMEM, HBM],
        out_specs=[VMEM] * 8,
        out_shape=SENT + [pltpu.VMEM(LOWER, bf16), pltpu.VMEM(UPPER, bf16)] * 2,
        scratch_shapes=[pltpu.VMEM((GROUP, WIDE, M + 128), f32), pltpu.SemaphoreType.DMA((2, PAIRS))],
        compiler_params=params(16),
        cost_estimate=cost(1 << 29, 8 * MIB),
        name="first_analysis",
    )(slot_orders, meta, in_vmem(spectra), in_hbm(legendre))
    return outs[:4], outs[4:6], outs[6:]


def second_analysis(slot_orders, meta, spectra, tables):
    return pl.pallas_call(
        second_analysis_kernel,
        in_specs=[SMEM, SMEM, VMEM, VMEM, VMEM],
        out_specs=[VMEM] * 4,
        out_shape=SENT,
        scratch_shapes=[pltpu.VMEM((GROUP, WIDE, M + 128), f32)],
        compiler_params=params(16),
        cost_estimate=cost(1 << 29, 4 * MIB),
        name="second_analysis",
    )(slot_orders, meta, in_vmem(spectra), *map(in_vmem, tables))


def respond(chunk, slot_orders, meta, response, own, arrived):
    return pl.pallas_call(
        functools.partial(respond_kernel, chunk),
        in_specs=[SMEM, SMEM] + [VMEM] * 5,
        out_specs=VMEM,
        out_shape=jax.ShapeDtypeStruct(PART, bf16),
        compiler_params=params(16),
        cost_estimate=cost(1 << 22, 2 * MIB),
        name="respond",
    )(slot_orders, meta, response, own, *arrived)


def synthesis(chunk, slot_orders, meta, coeffs, tables, earlier):
    return pl.pallas_call(
        functools.partial(synthesis_kernel, chunk),
        in_specs=[SMEM, SMEM] + [VMEM] * 6 + [HBM] * len(earlier),
        out_specs=HBM,
        out_shape=pltpu.HBM(SPECTRA, bf16),
        scratch_shapes=[
            pltpu.VMEM((GROUP, OWNERS, 2, ROWS, WIDE), bf16),
            pltpu.VMEM((GROUP, WIDE, M + 128), f32),
            pltpu.SemaphoreType.DMA((GROUP,)),
        ],
        input_output_aliases={8: 0} if earlier else {},
        compiler_params=params(16),
        cost_estimate=cost(1 << 29, 4 * MIB),
        name="synthesis",
    )(slot_orders, meta, *coeffs, *map(in_vmem, tables), *earlier)


def inverse(synthesized, table):
    return pl.pallas_call(
        inverse_kernel,
        in_specs=[VMEM, HBM],
        out_specs=HBM,
        out_shape=pltpu.HBM((2 * F, ROWS, NLON), bf16),
        scratch_shapes=[
            pltpu.VMEM((2, 2 * COLS, HALF), bf16),
            pltpu.VMEM((2, 2, 128 * ROWS, WIDE), f32),
            pltpu.VMEM((2, 4, 1024, 128), f32),
            pltpu.VMEM((2, 1024, 2 * COLS), bf16),
            pltpu.VMEM((1024, HALF), f32),
            pltpu.VMEM((2, 2, 2 * F, ROWS, TILE), bf16),
            pltpu.SemaphoreType.DMA((TILES,)),
            pltpu.SemaphoreType.DMA((2, 2)),
        ],
        compiler_params=params(36),
        cost_estimate=cost(4 << 30, 14 * MIB),
        name="inverse",
    )(in_vmem(synthesized), in_hbm(table))


def shards(ground_field, legendre, quad_weights, slot_orders, q_response):
    meta = jnp.stack([lax.axis_index("lat"), lax.axis_index("ord")]).astype(jnp.int32)
    first = slot_orders.reshape(COLS, 2)[:, 0]
    even = jnp.where((first & 1) == 0, first, M - 1 - first)
    response = jnp.transpose(q_response, (1, 0, 2))

    spectra = forward(quad_weights, even.reshape(1, COLS), ground_field.reshape(2 * F, ROWS, NLON))
    spectra = swap_owners(spectra)
    sums0, *tables = first_analysis(slot_orders, meta, spectra, legendre)
    sums1 = second_analysis(slot_orders, meta, spectra, tables[1])
    owns = [sums0[0], sums1[0]]
    partials = [exchange(sums0[1:]), exchange(sums1[1:])]
    coeffs = []
    for c in range(CHUNKS):
        induced = respond(c, slot_orders, meta, response, owns[c], partials[c])
        behind1, behind2, behind3 = exchange([induced] * 3)
        coeffs.append((induced, behind3, behind2, behind1))
    synthesized = []
    for c in range(CHUNKS):
        synthesized = [synthesis(c, slot_orders, meta, coeffs[c], tables[c], synthesized)]
    even, synthesized = lax.optimization_barrier((even, synthesized[0]))
    field = inverse(swap_owners(synthesized), turned_tables(even.reshape(COLS, 1)))
    return field.reshape(F, 2, ROWS, NLON)


def solution(mesh):
    in_specs = (
        P(None, None, ("lat", "ord"), None),
        P("ord", "lat", None),
        P(("lat", "ord")),
        P(),
        P(),
    )
    out_specs = P(None, None, ("lat", "ord"), None)
    return jax.shard_map(shards, mesh=mesh, in_specs=in_specs, out_specs=out_specs, check_vma=False)
```

```python
import functools
import math

import jax
import jax.numpy as jnp
from jax import lax
from jax.experimental import pallas as pl
from jax.experimental.pallas import tpu as pltpu
from jax.sharding import PartitionSpec as P

NLAT = 2048
NLON = 4096
HALF = 2048
M = 512
LMAX = 2047
F = 32
ROWS = 16
LATS = 4
OWNERS = 32
PAIRS = 8
CHUNKS = 2
GROUP = PAIRS // CHUNKS
COLS = OWNERS * PAIRS
WIDE = 128
PARTS = 4 * GROUP + 1
MIB = 1 << 20


def cos_sin(phase):
    quadrant = (phase + 512) >> 10
    x = (phase - (quadrant << 10)).astype(jnp.float32) * (2.0 * math.pi / NLON)
    y = x * x
    c = 1.0 + y * (-0.5 + y * (1.0 / 24 + y * (-1.0 / 720 + y * (1.0 / 40320))))
    s = x * (1.0 + y * (-1.0 / 6 + y * (1.0 / 120 + y * (-1.0 / 5040 + y * (1.0 / 362880)))))
    swap = (quadrant & 1) == 1
    cos = jnp.where(swap, s, c)
    sin = jnp.where(swap, c, s)
    cos = jnp.where(((quadrant + 1) & 2) == 2, -cos, cos)
    sin = jnp.where((quadrant & 2) == 2, -sin, sin)
    return cos, sin


def slot_order(even, parity):
    return LMAX + 1 - M + (even if parity == 0 else M - 1 - even)


def turned_table_kernel(even_ref, out_ref):
    for parity in range(2):
        order = slot_order(even_ref[...], parity)
        low = lax.broadcasted_iota(jnp.int32, (COLS, 128), 1)
        cb, sb = cos_sin((low * order) & (NLON - 1))
        high = lax.broadcasted_iota(jnp.int32, (COLS, 128), 1) & 15
        ca, sa = cos_sin((high * 128 * order) & (NLON - 1))
        for a in range(16):
            c1, s1 = ca[:, a : a + 1], sa[:, a : a + 1]
            lanes = slice(a * 128, (a + 1) * 128)
            out_ref[parity, :COLS, lanes] = (c1 * cb - s1 * sb).astype(jnp.bfloat16)
            out_ref[parity, COLS:, lanes] = (-(s1 * cb + c1 * sb)).astype(jnp.bfloat16)


def forward_kernel(
    weight_ref, even_ref, field_ref, out_ref, fields, folded, tables, sums, flat, packed, weights, field_sems, out_sems, weight_sem
):
    arrivals = [
        pltpu.make_async_copy(field_ref.at[pl.ds(16 * i, 16)], fields.at[pl.ds(16 * i, 16)], field_sems.at[i])
        for i in range(4)
    ]
    weight_copy = pltpu.make_async_copy(weight_ref, weights, weight_sem.at[0])
    for copy in arrivals + [weight_copy]:
        copy.start()

    def fill(parity, block):
        cols = slice(128 * block, 128 * block + 128)
        order = slot_order(even_ref[:, cols], parity)
        low = lax.broadcasted_iota(jnp.int32, (128, 128), 0)
        cb, sb = cos_sin((low * order) & (NLON - 1))
        high = lax.broadcasted_iota(jnp.int32, (16, 128), 0)
        ca, sa = cos_sin((high * 128 * order) & (NLON - 1))
        for a in range(16):
            c1, s1 = ca[a : a + 1], sa[a : a + 1]
            at = slice(a * 128, a * 128 + 128)
            tables[parity, block, at, :128] = (c1 * cb - s1 * sb).astype(jnp.bfloat16)
            tables[parity, block, at, 128:] = (-(s1 * cb + c1 * sb)).astype(jnp.bfloat16)

    for block in range(2):
        for parity in range(2):
            fill(parity, block)

    def multiply(parity, block, i):
        rows = slice(256 * i, 256 * i + 256)
        product = jnp.dot(folded[parity, rows, :], tables[parity, block], preferred_element_type=jnp.float32)
        for t in range(2):
            part = product[:, t * 128 : t * 128 + 128].reshape(8, 2, ROWS, 128)
            for c in range(2):
                sums[(2 * block + parity) % 2, :, i, t, c] = jnp.swapaxes(part[:, c], 0, 1)

    def turn(parity, block, k):
        factor = weights[k] * (1.0 / math.sqrt(NLON))
        flat[k] = (sums[(2 * block + parity) % 2, k].reshape(128, 128) * factor).T

    leaving = []

    def finish(parity, block):
        packed[block, parity] = jnp.swapaxes(flat[...], 0, 1).astype(jnp.bfloat16).reshape(16, PAIRS, ROWS, WIDE)
        leaving.append(
            pltpu.make_async_copy(
                packed.at[block, parity], out_ref.at[pl.ds(16 * block, 16), parity], out_sems.at[block, parity]
            )
        )
        leaving[-1].start()

    for i in range(4):
        rows = slice(256 * i, 256 * i + 256)
        arrivals[i].wait()
        field = fields[16 * i : 16 * i + 16].reshape(256, NLON)
        near, far = field[:, :HALF], field[:, HALF:]
        folded[0, rows, :] = near + far
        folded[1, rows, :] = near - far
        multiply(0, 0, i)

    weight_copy.wait()
    before = (0, 0)
    for block, parity in ((0, 1), (1, 0), (1, 1)):
        for i in range(4):
            multiply(parity, block, i)
            for k in range(4):
                turn(before[1], before[0], i * 4 + k)
        finish(before[1], before[0])
        before = (block, parity)
    for k in range(16):
        turn(1, 1, k)
    finish(1, 1)
    for copy in leaving:
        copy.wait()


def pair_facts(orders_ref, meta_ref, pair):
    first = orders_ref[(meta_ref[1] * PAIRS + pair) * 2]
    high_slot = jnp.where(first >= M // 2, 0, 1)
    lower = jnp.minimum(first, M - 1 - first)
    high_parity = (M - 1 - lower) & 1
    return high_slot, high_parity, lower


def legendre_copies(orders_ref, meta_ref, legendre_ref, tables, sems):
    copies = []
    for p in range(PAIRS):
        high_slot, _, _ = pair_facts(orders_ref, meta_ref, p)
        low, high = tables[2 * (p // GROUP)].at[p % GROUP], tables[2 * (p // GROUP) + 1].at[p % GROUP]
        copies.append(
            (
                pltpu.make_async_copy(legendre_ref.at[2 * p + 1 - high_slot], low, sems.at[0, p]),
                pltpu.make_async_copy(legendre_ref.at[2 * p + high_slot, :, pl.ds(M // 2, M // 2)], high, sems.at[1, p]),
            )
        )
    return copies


def first_analysis_kernel(orders_ref, meta_ref, spec_ref, legendre_ref, *refs):
    outs, tables, (whole, sems) = refs[:4], refs[4:8], refs[8:]
    copies = legendre_copies(orders_ref, meta_ref, legendre_ref, tables, sems)
    for pair in copies:
        for copy in pair:
            copy.start()
    analyse(0, orders_ref, meta_ref, spec_ref, tables[0], tables[1], outs, whole, copies)
    for pair in copies[GROUP:]:
        for copy in pair:
            copy.wait()


def second_analysis_kernel(orders_ref, meta_ref, spec_ref, low_ref, high_ref, *refs):
    analyse(1, orders_ref, meta_ref, spec_ref, low_ref, high_ref, refs[:4], refs[4], ())


def analyse(chunk, orders_ref, meta_ref, spec_ref, low_ref, high_ref, outs, whole, copies):
    dims = (((0,), (0,)), ((), ()))
    lane = lax.broadcasted_iota(jnp.int32, (WIDE, 256), 1)
    lane1 = lax.broadcasted_iota(jnp.int32, (WIDE, 128), 1)
    extras = jnp.zeros((WIDE, 128), jnp.float32)
    for p in range(GROUP):
        pair = chunk * GROUP + p
        _, high_parity, lower = pair_facts(orders_ref, meta_ref, pair)
        for copy in copies[p] if copies else ():
            copy.wait()
        low_spec = spec_ref[:, 1 - high_parity, pair].reshape(M, WIDE)
        high_spec = spec_ref[:, high_parity, pair].reshape(M, WIDE)
        low = lax.dot_general(low_spec, low_ref[p], dims, preferred_element_type=jnp.float32)
        high = lax.dot_general(high_spec, high_ref[p], dims, preferred_element_type=jnp.float32)
        moved = pltpu.roll(low[:, :256], (256 - lower) & 255, 1)
        whole[p, :, :256] = low[:, 256:]
        whole[p, :, 256:512] = jnp.where(lane < 255 - lower, moved, high)
        extras = jnp.where(lane1 == p, pltpu.roll(low[:, 128:256], p + 1, 1), extras)
        if p == GROUP - 1:
            whole[p, :, 512:] = extras
        for d, out in enumerate(outs):
            rows = pl.ds(pl.multiple_of(((meta_ref[0] + d) & 3) * 32, 32), 32)
            for part in range(5 if p == GROUP - 1 else 4):
                out[4 * p + part] = whole[p, rows, part * 128 : part * 128 + 128].astype(out.dtype)


def respond_kernel(chunk, orders_ref, meta_ref, q_ref, own, r1, r2, r3, out):
    block = pl.ds(pl.multiple_of(meta_ref[0] * 8, 8), 8)
    scale = 1.0 / math.sqrt(NLAT)

    def respond(part, qr, qi):
        total = own[part] + r1[part].astype(jnp.float32)
        total = total + r2[part].astype(jnp.float32) + r3[part].astype(jnp.float32)
        total = total * scale
        pieces = []
        for t in range(2):
            real, imag = total[16 * t : 16 * t + 8], total[16 * t + 8 : 16 * t + 16]
            pieces += [qr * real - qi * imag, qr * imag + qi * real]
        out[part] = jnp.concatenate(pieces, axis=0).astype(jnp.bfloat16)

    qr, qi = q_ref[0, block, :], q_ref[1, block, :]
    lane = lax.broadcasted_iota(jnp.int32, (8, 256), 1)
    for p in range(GROUP):
        _, _, lower = pair_facts(orders_ref, meta_ref, chunk * GROUP + p)
        shift = (256 - lower) & 255
        merged = [
            jnp.where(lane < 255 - lower, pltpu.roll(q[:, :256], shift, 1), q[:, 256:]) for q in (qr, qi)
        ]
        for part in range(2):
            lanes = slice(part * 128, part * 128 + 128)
            respond(4 * p + part, qr[:, 256:][:, lanes], qi[:, 256:][:, lanes])
            respond(4 * p + 2 + part, merged[0][:, lanes], merged[1][:, lanes])
    respond(
        PARTS - 1,
        jnp.broadcast_to(qr[:, 255:256], (8, 128)),
        jnp.broadcast_to(qi[:, 255:256], (8, 128)),
    )


def synthesis_kernel(chunk, orders_ref, meta_ref, c0, c1, c2, c3, low_ref, high_ref, *refs):
    out_ref, packed, whole, sems = refs[-4:]
    dims = (((1,), (1,)), ((), ()))
    scale = 1.0 / math.sqrt(M)
    lane = lax.broadcasted_iota(jnp.int32, (WIDE, 256), 1)
    copies = []
    for p in range(GROUP):
        pair = chunk * GROUP + p
        _, high_parity, lower = pair_facts(orders_ref, meta_ref, pair)
        for d, coeff in enumerate((c0, c1, c2, c3)):
            rows = pl.ds(pl.multiple_of(((meta_ref[0] + d) & 3) * 32, 32), 32)
            for part in range(4):
                whole[p, rows, part * 128 : part * 128 + 128] = coeff[4 * p + part].astype(jnp.float32)
            if p == 0:
                whole[0, rows, 512:640] = coeff[PARTS - 1].astype(jnp.float32)
        merged = whole[p, :, 256:512]
        moved = pltpu.roll(merged, lower, 1)
        extra = pltpu.roll(whole[0, :, 512:640], 127 - p, 1)
        extra = jnp.concatenate([extra, extra], axis=1)
        head = jnp.where(lane == 255, extra, jnp.where(lane >= lower, moved, 0.0))
        low = jnp.concatenate([head.astype(jnp.bfloat16), whole[p, :, :256].astype(jnp.bfloat16)], axis=1)
        high = jnp.where(lane >= 255 - lower, merged, 0.0).astype(jnp.bfloat16)
        low_out = lax.dot_general(low_ref[p], low, dims, preferred_element_type=jnp.float32)
        high_out = lax.dot_general(high_ref[p], high, dims, preferred_element_type=jnp.float32)
        packed[p, :, 1 - high_parity] = (low_out * scale).astype(jnp.bfloat16).reshape(OWNERS, ROWS, WIDE)
        packed[p, :, high_parity] = (high_out * scale).astype(jnp.bfloat16).reshape(OWNERS, ROWS, WIDE)
        copies.append(pltpu.make_async_copy(packed.at[p], out_ref.at[:, :, pair], sems.at[p]))
        copies[-1].start()
    for copy in copies:
        copy.wait()


TILE = 512
BAND = 512
TILES = HALF // TILE


def inverse_kernel(
    synth_ref, table_ref, out_ref, tables, loose, turned, left, evens, packed, table_sems, out_sems
):
    arrivals = []
    for i in range(TILES):
        lanes = pl.ds(i * TILE, TILE)
        arrivals.append(pltpu.make_async_copy(table_ref.at[:, :, lanes], tables.at[:, :, lanes], table_sems.at[i]))
        arrivals[i].start()

    def loosen(parity, block, k):
        values = loose[parity, block, k].T * (1.0 / math.sqrt(2 * M))
        turned[parity, block, k] = values

    def widen(parity):
        for block in range(2):
            values = synth_ref[16 * block : 16 * block + 16, parity].reshape(128, ROWS, WIDE).astype(jnp.float32)
            loose[parity, block] = jnp.swapaxes(values, 0, 1)

    def narrow(parity):
        for block in range(2):
            for at in range(16):
                high, t, c = at // 4, at // 2 % 2, at % 2
                rows = jnp.swapaxes(turned[parity, block, :, 8 * at : 8 * at + 8, :], 0, 1).astype(jnp.bfloat16)
                lanes = slice(t * COLS + block * 128, t * COLS + block * 128 + 128)
                left[parity, 8 * high : 8 * high + 8, c, :, lanes] = rows

    widen(0)
    for block in range(2):
        for k in range(ROWS):
            loosen(0, block, k)
    narrow(0)
    widen(1)
    for i in range(TILES):
        lanes = slice(i * TILE, i * TILE + TILE)
        arrivals[i].wait()
        for r in range(0, 1024, BAND):
            rows = slice(r, r + BAND)
            evens[rows, lanes] = jnp.dot(left[0].reshape(1024, 2 * COLS)[rows, :], tables[0, :, lanes], preferred_element_type=jnp.float32)
        for block in range(2):
            for k in range(ROWS // TILES):
                loosen(1, block, i * (ROWS // TILES) + k)
    narrow(1)
    leaving = []
    for i in range(TILES):
        slot = i % 2
        lanes = slice(i * TILE, i * TILE + TILE)
        if i >= 2:
            for copy in leaving[2 * i - 4 : 2 * i - 2]:
                copy.wait()
        for r in range(0, 1024, BAND):
            rows = slice(r, r + BAND)
            even = evens[rows, lanes]
            odd = jnp.dot(left[1].reshape(1024, 2 * COLS)[rows, :], tables[1, :, lanes], preferred_element_type=jnp.float32)
            at = slice(r // ROWS, (r + BAND) // ROWS)
            packed[slot, 0, at] = (even + odd).astype(jnp.bfloat16).reshape(BAND // ROWS, ROWS, TILE)
            packed[slot, 1, at] = (even - odd).astype(jnp.bfloat16).reshape(BAND // ROWS, ROWS, TILE)
        for side in range(2):
            copy = pltpu.make_async_copy(
                packed.at[slot, side], out_ref.at[:, :, pl.ds(side * HALF + i * TILE, TILE)], out_sems.at[slot, side]
            )
            copy.start()
            leaving.append(copy)
    for copy in leaving[-4:]:
        copy.wait()


def params(mib=56):
    return pltpu.CompilerParams(vmem_limit_bytes=mib * MIB)


def cost(flops, size):
    return pl.CostEstimate(flops=flops, bytes_accessed=size, transcendentals=0)


def in_hbm(x):
    return pltpu.with_memory_space_constraint(x, pltpu.HBM)


def in_vmem(x):
    return pltpu.with_memory_space_constraint(x, pltpu.VMEM)


SMEM = pl.BlockSpec(memory_space=pltpu.SMEM)
VMEM = pl.BlockSpec(memory_space=pltpu.VMEM)
HBM = pl.BlockSpec(memory_space=pltpu.HBM)
ANY = pl.BlockSpec(memory_space=pl.ANY)
SPECTRA = (OWNERS, 2, PAIRS, ROWS, WIDE)
PART = (PARTS, 32, 128)
LOWER, UPPER = (GROUP, M, M), (GROUP, M, M // 2)
bf16, f32 = jnp.bfloat16, jnp.float32


def exchange(parts):
    return [lax.ppermute(part, "lat", [(i, (i + d) % LATS) for i in range(LATS)]) for d, part in zip((1, 2, 3), parts)]


def swap_owners(values):
    return lax.all_to_all(values, "ord", split_axis=0, concat_axis=0, tiled=True)


def forward(quad_weights, even, field):
    return pl.pallas_call(
        forward_kernel,
        in_specs=[HBM, VMEM, HBM],
        out_specs=HBM,
        out_shape=pltpu.HBM(SPECTRA, bf16),
        scratch_shapes=[
            pltpu.VMEM((2 * F, ROWS, NLON), bf16),
            pltpu.VMEM((2, 1024, HALF), bf16),
            pltpu.VMEM((2, 2, HALF, 256), bf16),
            pltpu.VMEM((2, ROWS, 4, 2, 2, 8, 128), f32),
            pltpu.VMEM((ROWS, 128, WIDE), f32),
            pltpu.VMEM((2, 2, 16, PAIRS, ROWS, WIDE), bf16),
            pltpu.SMEM((ROWS,), f32),
            pltpu.SemaphoreType.DMA((4,)),
            pltpu.SemaphoreType.DMA((2, 2)),
            pltpu.SemaphoreType.DMA((1,)),
        ],
        compiler_params=params(40),
        cost_estimate=cost(4 << 30, 10 * MIB),
        name="forward",
    )(in_hbm(quad_weights), even, in_hbm(field))


def turned_tables(even):
    return pl.pallas_call(
        turned_table_kernel,
        in_specs=[VMEM],
        out_specs=VMEM,
        out_shape=pltpu.HBM((2, 2 * COLS, HALF), bf16),
        compiler_params=params(16),
        cost_estimate=cost(1 << 26, 4 * MIB),
        name="turned_table",
    )(even)


SENT = [jax.ShapeDtypeStruct(PART, f32)] + [jax.ShapeDtypeStruct(PART, bf16)] * 3


def first_analysis(slot_orders, meta, spectra, legendre):
    outs = pl.pallas_call(
        first_analysis_kernel,
        in_specs=[SMEM, SMEM, VMEM, HBM],
        out_specs=[VMEM] * 8,
        out_shape=SENT + [pltpu.VMEM(LOWER, bf16), pltpu.VMEM(UPPER, bf16)] * 2,
        scratch_shapes=[pltpu.VMEM((GROUP, WIDE, M + 128), f32), pltpu.SemaphoreType.DMA((2, PAIRS))],
        compiler_params=params(16),
        cost_estimate=cost(1 << 29, 8 * MIB),
        name="first_analysis",
    )(slot_orders, meta, in_vmem(spectra), in_hbm(legendre))
    return outs[:4], outs[4:6], outs[6:]


def second_analysis(slot_orders, meta, spectra, tables):
    return pl.pallas_call(
        second_analysis_kernel,
        in_specs=[SMEM, SMEM, VMEM, VMEM, VMEM],
        out_specs=[VMEM] * 4,
        out_shape=SENT,
        scratch_shapes=[pltpu.VMEM((GROUP, WIDE, M + 128), f32)],
        compiler_params=params(16),
        cost_estimate=cost(1 << 29, 4 * MIB),
        name="second_analysis",
    )(slot_orders, meta, in_vmem(spectra), *map(in_vmem, tables))


def respond(chunk, slot_orders, meta, response, own, arrived):
    return pl.pallas_call(
        functools.partial(respond_kernel, chunk),
        in_specs=[SMEM, SMEM] + [VMEM] * 5,
        out_specs=VMEM,
        out_shape=jax.ShapeDtypeStruct(PART, bf16),
        compiler_params=params(16),
        cost_estimate=cost(1 << 22, 2 * MIB),
        name="respond",
    )(slot_orders, meta, response, own, *arrived)


def synthesis(chunk, slot_orders, meta, coeffs, tables, earlier):
    return pl.pallas_call(
        functools.partial(synthesis_kernel, chunk),
        in_specs=[SMEM, SMEM] + [VMEM] * 6 + [HBM] * len(earlier),
        out_specs=HBM,
        out_shape=pltpu.HBM(SPECTRA, bf16),
        scratch_shapes=[
            pltpu.VMEM((GROUP, OWNERS, 2, ROWS, WIDE), bf16),
            pltpu.VMEM((GROUP, WIDE, M + 128), f32),
            pltpu.SemaphoreType.DMA((GROUP,)),
        ],
        input_output_aliases={8: 0} if earlier else {},
        compiler_params=params(16),
        cost_estimate=cost(1 << 29, 4 * MIB),
        name="synthesis",
    )(slot_orders, meta, *coeffs, *map(in_vmem, tables), *earlier)


def inverse(synthesized, table):
    return pl.pallas_call(
        inverse_kernel,
        in_specs=[VMEM, HBM],
        out_specs=HBM,
        out_shape=pltpu.HBM((2 * F, ROWS, NLON), bf16),
        scratch_shapes=[
            pltpu.VMEM((2, 2 * COLS, HALF), bf16),
            pltpu.VMEM((2, 2, ROWS, 128, WIDE), f32),
            pltpu.VMEM((2, 2, ROWS, 128, 128), f32),
            pltpu.VMEM((2, F, 2, ROWS, 2 * COLS), bf16),
            pltpu.VMEM((1024, HALF), f32),
            pltpu.VMEM((2, 2, 2 * F, ROWS, TILE), bf16),
            pltpu.SemaphoreType.DMA((TILES,)),
            pltpu.SemaphoreType.DMA((2, 2)),
        ],
        compiler_params=params(36),
        cost_estimate=cost(4 << 30, 14 * MIB),
        name="inverse",
    )(in_vmem(synthesized), in_hbm(table))


def shards(ground_field, legendre, quad_weights, slot_orders, q_response):
    meta = jnp.stack([lax.axis_index("lat"), lax.axis_index("ord")]).astype(jnp.int32)
    first = slot_orders.reshape(COLS, 2)[:, 0]
    even = jnp.where((first & 1) == 0, first, M - 1 - first)
    response = jnp.transpose(q_response, (1, 0, 2))

    spectra = forward(quad_weights, even.reshape(1, COLS), ground_field.reshape(2 * F, ROWS, NLON))
    spectra = swap_owners(spectra)
    sums0, *tables = first_analysis(slot_orders, meta, spectra, legendre)
    sums1 = second_analysis(slot_orders, meta, spectra, tables[1])
    owns = [sums0[0], sums1[0]]
    partials = [exchange(sums0[1:]), exchange(sums1[1:])]
    coeffs = []
    for c in range(CHUNKS):
        induced = respond(c, slot_orders, meta, response, owns[c], partials[c])
        behind1, behind2, behind3 = exchange([induced] * 3)
        coeffs.append((induced, behind3, behind2, behind1))
    synthesized = []
    for c in range(CHUNKS):
        synthesized = [synthesis(c, slot_orders, meta, coeffs[c], tables[c], synthesized)]
    even, synthesized = lax.optimization_barrier((even, synthesized[0]))
    field = inverse(swap_owners(synthesized), turned_tables(even.reshape(COLS, 1)))
    return field.reshape(F, 2, ROWS, NLON)


def solution(mesh):
    in_specs = (
        P(None, None, ("lat", "ord"), None),
        P("ord", "lat", None),
        P(("lat", "ord")),
        P(),
        P(),
    )
    out_specs = P(None, None, ("lat", "ord"), None)
    return jax.shard_map(shards, mesh=mesh, in_specs=in_specs, out_specs=out_specs, check_vma=False)
```

```python
import functools
import math

import jax
import jax.numpy as jnp
from jax import lax
from jax.experimental import pallas as pl
from jax.experimental.pallas import tpu as pltpu
from jax.sharding import PartitionSpec as P

NLAT = 2048
NLON = 4096
HALF = 2048
M = 512
LMAX = 2047
F = 32
ROWS = 16
LATS = 4
OWNERS = 32
PAIRS = 8
CHUNKS = 2
GROUP = PAIRS // CHUNKS
COLS = OWNERS * PAIRS
WIDE = 128
PARTS = 4 * GROUP + 1
MIB = 1 << 20


def cos_sin(phase):
    quadrant = (phase + 512) >> 10
    x = (phase - (quadrant << 10)).astype(jnp.float32) * (2.0 * math.pi / NLON)
    y = x * x
    c = 1.0 + y * (-0.5 + y * (1.0 / 24 + y * (-1.0 / 720 + y * (1.0 / 40320))))
    s = x * (1.0 + y * (-1.0 / 6 + y * (1.0 / 120 + y * (-1.0 / 5040 + y * (1.0 / 362880)))))
    swap = (quadrant & 1) == 1
    cos = jnp.where(swap, s, c)
    sin = jnp.where(swap, c, s)
    cos = jnp.where(((quadrant + 1) & 2) == 2, -cos, cos)
    sin = jnp.where((quadrant & 2) == 2, -sin, sin)
    return cos, sin


def slot_order(even, parity):
    return LMAX + 1 - M + (even if parity == 0 else M - 1 - even)


def turned_table_kernel(even_ref, out_ref):
    for parity in range(2):
        order = slot_order(even_ref[...], parity)
        low = lax.broadcasted_iota(jnp.int32, (COLS, 128), 1)
        cb, sb = cos_sin((low * order) & (NLON - 1))
        high = lax.broadcasted_iota(jnp.int32, (COLS, 128), 1) & 15
        ca, sa = cos_sin((high * 128 * order) & (NLON - 1))
        for a in range(16):
            c1, s1 = ca[:, a : a + 1], sa[:, a : a + 1]
            lanes = slice(a * 128, (a + 1) * 128)
            out_ref[parity, :COLS, lanes] = (c1 * cb - s1 * sb).astype(jnp.bfloat16)
            out_ref[parity, COLS:, lanes] = (-(s1 * cb + c1 * sb)).astype(jnp.bfloat16)


def forward_kernel(
    weight_ref, even_ref, field_ref, out_ref, fields, folded, tables, sums, flat, packed, weights, field_sems, out_sems, weight_sem
):
    arrivals = [
        pltpu.make_async_copy(field_ref.at[pl.ds(16 * i, 16)], fields.at[pl.ds(16 * i, 16)], field_sems.at[i])
        for i in range(4)
    ]
    weight_copy = pltpu.make_async_copy(weight_ref, weights, weight_sem.at[0])
    for copy in arrivals + [weight_copy]:
        copy.start()

    def fill(parity, block):
        cols = slice(128 * block, 128 * block + 128)
        order = slot_order(even_ref[:, cols], parity)
        low = lax.broadcasted_iota(jnp.int32, (128, 128), 0)
        cb, sb = cos_sin((low * order) & (NLON - 1))
        high = lax.broadcasted_iota(jnp.int32, (16, 128), 0)
        ca, sa = cos_sin((high * 128 * order) & (NLON - 1))
        for a in range(16):
            c1, s1 = ca[a : a + 1], sa[a : a + 1]
            at = slice(a * 128, a * 128 + 128)
            tables[parity, block, at, :128] = (c1 * cb - s1 * sb).astype(jnp.bfloat16)
            tables[parity, block, at, 128:] = (-(s1 * cb + c1 * sb)).astype(jnp.bfloat16)

    for block in range(2):
        for parity in range(2):
            fill(parity, block)

    def multiply(parity, block, i):
        rows = slice(256 * i, 256 * i + 256)
        product = jnp.dot(folded[parity, rows, :], tables[parity, block], preferred_element_type=jnp.float32)
        for t in range(2):
            part = product[:, t * 128 : t * 128 + 128].reshape(8, 2, ROWS, 128)
            for c in range(2):
                sums[(2 * block + parity) % 2, :, i, t, c] = jnp.swapaxes(part[:, c], 0, 1)

    def turn(parity, block, k):
        factor = weights[k] * (1.0 / math.sqrt(NLON))
        flat[k] = (sums[(2 * block + parity) % 2, k].reshape(128, 128) * factor).T

    leaving = []

    def finish(parity, block):
        packed[block, parity] = jnp.swapaxes(flat[...], 0, 1).astype(jnp.bfloat16).reshape(16, PAIRS, ROWS, WIDE)
        leaving.append(
            pltpu.make_async_copy(
                packed.at[block, parity], out_ref.at[pl.ds(16 * block, 16), parity], out_sems.at[block, parity]
            )
        )
        leaving[-1].start()

    for i in range(4):
        rows = slice(256 * i, 256 * i + 256)
        arrivals[i].wait()
        field = fields[16 * i : 16 * i + 16].reshape(256, NLON)
        near, far = field[:, :HALF], field[:, HALF:]
        folded[0, rows, :] = near + far
        folded[1, rows, :] = near - far
        multiply(0, 0, i)

    weight_copy.wait()
    before = (0, 0)
    for block, parity in ((0, 1), (1, 0), (1, 1)):
        for i in range(4):
            multiply(parity, block, i)
            for k in range(4):
                turn(before[1], before[0], i * 4 + k)
        finish(before[1], before[0])
        before = (block, parity)
    for k in range(16):
        turn(1, 1, k)
    finish(1, 1)
    for copy in leaving:
        copy.wait()


def pair_facts(orders_ref, meta_ref, pair):
    first = orders_ref[(meta_ref[1] * PAIRS + pair) * 2]
    high_slot = jnp.where(first >= M // 2, 0, 1)
    lower = jnp.minimum(first, M - 1 - first)
    high_parity = (M - 1 - lower) & 1
    return high_slot, high_parity, lower


def legendre_copies(orders_ref, meta_ref, legendre_ref, tables, sems):
    copies = []
    for p in range(PAIRS):
        high_slot, _, _ = pair_facts(orders_ref, meta_ref, p)
        low, high = tables[2 * (p // GROUP)].at[p % GROUP], tables[2 * (p // GROUP) + 1].at[p % GROUP]
        copies.append(
            (
                pltpu.make_async_copy(legendre_ref.at[2 * p + 1 - high_slot], low, sems.at[0, p]),
                pltpu.make_async_copy(legendre_ref.at[2 * p + high_slot, :, pl.ds(M // 2, M // 2)], high, sems.at[1, p]),
            )
        )
    return copies


def first_analysis_kernel(orders_ref, meta_ref, spec_ref, legendre_ref, *refs):
    outs, tables, (whole, sems) = refs[:4], refs[4:8], refs[8:]
    copies = legendre_copies(orders_ref, meta_ref, legendre_ref, tables, sems)
    for pair in copies:
        for copy in pair:
            copy.start()
    analyse(0, orders_ref, meta_ref, spec_ref, tables[0], tables[1], outs, whole, copies)
    for pair in copies[GROUP:]:
        for copy in pair:
            copy.wait()


def second_analysis_kernel(orders_ref, meta_ref, spec_ref, low_ref, high_ref, *refs):
    analyse(1, orders_ref, meta_ref, spec_ref, low_ref, high_ref, refs[:4], refs[4], ())


def analyse(chunk, orders_ref, meta_ref, spec_ref, low_ref, high_ref, outs, whole, copies):
    dims = (((0,), (0,)), ((), ()))
    lane = lax.broadcasted_iota(jnp.int32, (WIDE, 256), 1)
    lane1 = lax.broadcasted_iota(jnp.int32, (WIDE, 128), 1)
    extras = jnp.zeros((WIDE, 128), jnp.float32)
    for p in range(GROUP):
        pair = chunk * GROUP + p
        _, high_parity, lower = pair_facts(orders_ref, meta_ref, pair)
        for copy in copies[p] if copies else ():
            copy.wait()
        low_spec = spec_ref[:, 1 - high_parity, pair].reshape(M, WIDE)
        high_spec = spec_ref[:, high_parity, pair].reshape(M, WIDE)
        low = lax.dot_general(low_spec, low_ref[p], dims, preferred_element_type=jnp.float32)
        high = lax.dot_general(high_spec, high_ref[p], dims, preferred_element_type=jnp.float32)
        moved = pltpu.roll(low[:, :256], (256 - lower) & 255, 1)
        whole[p, :, :256] = low[:, 256:]
        whole[p, :, 256:512] = jnp.where(lane < 255 - lower, moved, high)
        extras = jnp.where(lane1 == p, pltpu.roll(low[:, 128:256], p + 1, 1), extras)
        if p == GROUP - 1:
            whole[p, :, 512:] = extras
        for d, out in enumerate(outs):
            rows = pl.ds(pl.multiple_of(((meta_ref[0] + d) & 3) * 32, 32), 32)
            for part in range(5 if p == GROUP - 1 else 4):
                out[4 * p + part] = whole[p, rows, part * 128 : part * 128 + 128].astype(out.dtype)


def respond_kernel(chunk, orders_ref, meta_ref, q_ref, own, r1, r2, r3, out):
    block = pl.ds(pl.multiple_of(meta_ref[0] * 8, 8), 8)
    scale = 1.0 / math.sqrt(NLAT)

    def respond(part, qr, qi):
        total = own[part] + r1[part].astype(jnp.float32)
        total = total + r2[part].astype(jnp.float32) + r3[part].astype(jnp.float32)
        total = total * scale
        pieces = []
        for t in range(2):
            real, imag = total[16 * t : 16 * t + 8], total[16 * t + 8 : 16 * t + 16]
            pieces += [qr * real - qi * imag, qr * imag + qi * real]
        out[part] = jnp.concatenate(pieces, axis=0).astype(jnp.bfloat16)

    qr, qi = q_ref[0, block, :], q_ref[1, block, :]
    lane = lax.broadcasted_iota(jnp.int32, (8, 256), 1)
    for p in range(GROUP):
        _, _, lower = pair_facts(orders_ref, meta_ref, chunk * GROUP + p)
        shift = (256 - lower) & 255
        merged = [
            jnp.where(lane < 255 - lower, pltpu.roll(q[:, :256], shift, 1), q[:, 256:]) for q in (qr, qi)
        ]
        for part in range(2):
            lanes = slice(part * 128, part * 128 + 128)
            respond(4 * p + part, qr[:, 256:][:, lanes], qi[:, 256:][:, lanes])
            respond(4 * p + 2 + part, merged[0][:, lanes], merged[1][:, lanes])
    respond(
        PARTS - 1,
        jnp.broadcast_to(qr[:, 255:256], (8, 128)),
        jnp.broadcast_to(qi[:, 255:256], (8, 128)),
    )


def synthesis_kernel(chunk, orders_ref, meta_ref, c0, c1, c2, c3, low_ref, high_ref, *refs):
    out_ref, packed, whole, sems = refs[-4:]
    dims = (((1,), (1,)), ((), ()))
    scale = 1.0 / math.sqrt(M)
    lane = lax.broadcasted_iota(jnp.int32, (WIDE, 256), 1)
    copies = []
    for p in range(GROUP):
        pair = chunk * GROUP + p
        _, high_parity, lower = pair_facts(orders_ref, meta_ref, pair)
        for d, coeff in enumerate((c0, c1, c2, c3)):
            rows = pl.ds(pl.multiple_of(((meta_ref[0] + d) & 3) * 32, 32), 32)
            for part in range(4):
                whole[p, rows, part * 128 : part * 128 + 128] = coeff[4 * p + part].astype(jnp.float32)
            if p == 0:
                whole[0, rows, 512:640] = coeff[PARTS - 1].astype(jnp.float32)
        merged = whole[p, :, 256:512]
        moved = pltpu.roll(merged, lower, 1)
        extra = pltpu.roll(whole[0, :, 512:640], 127 - p, 1)
        extra = jnp.concatenate([extra, extra], axis=1)
        head = jnp.where(lane == 255, extra, jnp.where(lane >= lower, moved, 0.0))
        low = jnp.concatenate([head.astype(jnp.bfloat16), whole[p, :, :256].astype(jnp.bfloat16)], axis=1)
        high = jnp.where(lane >= 255 - lower, merged, 0.0).astype(jnp.bfloat16)
        low_out = lax.dot_general(low_ref[p], low, dims, preferred_element_type=jnp.float32)
        high_out = lax.dot_general(high_ref[p], high, dims, preferred_element_type=jnp.float32)
        packed[p, :, 1 - high_parity] = (low_out * scale).astype(jnp.bfloat16).reshape(OWNERS, ROWS, WIDE)
        packed[p, :, high_parity] = (high_out * scale).astype(jnp.bfloat16).reshape(OWNERS, ROWS, WIDE)
        copies.append(pltpu.make_async_copy(packed.at[p], out_ref.at[:, :, pair], sems.at[p]))
        copies[-1].start()
    for copy in copies:
        copy.wait()


TILE = 512
BAND = 512
TILES = HALF // TILE


def inverse_kernel(
    synth_ref, table_ref, out_ref, tables, loose, turned, left, evens, packed, table_sems, out_sems
):
    arrivals = []
    for i in range(TILES):
        lanes = pl.ds(i * TILE, TILE)
        arrivals.append(pltpu.make_async_copy(table_ref.at[:, :, lanes], tables.at[:, :, lanes], table_sems.at[i]))
        arrivals[i].start()

    def loosen(parity, block, k):
        values = loose[parity, block, k].T * (1.0 / math.sqrt(2 * M))
        turned[parity, block, k] = values

    def widen(parity):
        for block in range(2):
            values = synth_ref[16 * block : 16 * block + 16, parity].reshape(128, ROWS, WIDE).astype(jnp.float32)
            loose[parity, block] = jnp.swapaxes(values, 0, 1)

    def narrow(parity):
        for block in range(2):
            for at in range(16):
                high, t, c = at // 4, at // 2 % 2, at % 2
                rows = jnp.swapaxes(turned[parity, block, :, 8 * at : 8 * at + 8, :], 0, 1).astype(jnp.bfloat16)
                lanes = slice(t * COLS + block * 128, t * COLS + block * 128 + 128)
                left[parity, 8 * high : 8 * high + 8, c, :, lanes] = rows

    widen(0)
    for block in range(2):
        for k in range(ROWS):
            loosen(0, block, k)
    narrow(0)
    widen(1)
    for i in range(TILES):
        lanes = slice(i * TILE, i * TILE + TILE)
        arrivals[i].wait()
        for r in range(0, 1024, BAND):
            rows = slice(r, r + BAND)
            evens[rows, lanes] = jnp.dot(left[0].reshape(1024, 2 * COLS)[rows, :], tables[0, :, lanes], preferred_element_type=jnp.float32)
        for block in range(2):
            for k in range(ROWS // TILES):
                loosen(1, block, i * (ROWS // TILES) + k)
    narrow(1)
    leaving = []
    for i in range(TILES):
        slot = i % 2
        lanes = slice(i * TILE, i * TILE + TILE)
        if i >= 2:
            for copy in leaving[4 * i - 8 : 4 * i - 4]:
                copy.wait()
        for r in range(0, 1024, BAND):
            rows = slice(r, r + BAND)
            even = evens[rows, lanes]
            odd = jnp.dot(left[1].reshape(1024, 2 * COLS)[rows, :], tables[1, :, lanes], preferred_element_type=jnp.float32)
            at = slice(r // ROWS, (r + BAND) // ROWS)
            packed[slot, 0, at] = (even + odd).astype(jnp.bfloat16).reshape(BAND // ROWS, ROWS, TILE)
            packed[slot, 1, at] = (even - odd).astype(jnp.bfloat16).reshape(BAND // ROWS, ROWS, TILE)
            for side in range(2):
                band = pl.ds(r // ROWS, BAND // ROWS)
                copy = pltpu.make_async_copy(
                    packed.at[slot, side, band],
                    out_ref.at[band, :, pl.ds(side * HALF + i * TILE, TILE)],
                    out_sems.at[slot, side, r // BAND],
                )
                copy.start()
                leaving.append(copy)
    for copy in leaving[-8:]:
        copy.wait()


def params(mib=56):
    return pltpu.CompilerParams(vmem_limit_bytes=mib * MIB)


def cost(flops, size):
    return pl.CostEstimate(flops=flops, bytes_accessed=size, transcendentals=0)


def in_hbm(x):
    return pltpu.with_memory_space_constraint(x, pltpu.HBM)


def in_vmem(x):
    return pltpu.with_memory_space_constraint(x, pltpu.VMEM)


SMEM = pl.BlockSpec(memory_space=pltpu.SMEM)
VMEM = pl.BlockSpec(memory_space=pltpu.VMEM)
HBM = pl.BlockSpec(memory_space=pltpu.HBM)
ANY = pl.BlockSpec(memory_space=pl.ANY)
SPECTRA = (OWNERS, 2, PAIRS, ROWS, WIDE)
PART = (PARTS, 32, 128)
LOWER, UPPER = (GROUP, M, M), (GROUP, M, M // 2)
bf16, f32 = jnp.bfloat16, jnp.float32


def exchange(parts):
    return [lax.ppermute(part, "lat", [(i, (i + d) % LATS) for i in range(LATS)]) for d, part in zip((1, 2, 3), parts)]


def swap_owners(values):
    return lax.all_to_all(values, "ord", split_axis=0, concat_axis=0, tiled=True)


def forward(quad_weights, even, field):
    return pl.pallas_call(
        forward_kernel,
        in_specs=[HBM, VMEM, HBM],
        out_specs=HBM,
        out_shape=pltpu.HBM(SPECTRA, bf16),
        scratch_shapes=[
            pltpu.VMEM((2 * F, ROWS, NLON), bf16),
            pltpu.VMEM((2, 1024, HALF), bf16),
            pltpu.VMEM((2, 2, HALF, 256), bf16),
            pltpu.VMEM((2, ROWS, 4, 2, 2, 8, 128), f32),
            pltpu.VMEM((ROWS, 128, WIDE), f32),
            pltpu.VMEM((2, 2, 16, PAIRS, ROWS, WIDE), bf16),
            pltpu.SMEM((ROWS,), f32),
            pltpu.SemaphoreType.DMA((4,)),
            pltpu.SemaphoreType.DMA((2, 2)),
            pltpu.SemaphoreType.DMA((1,)),
        ],
        compiler_params=params(40),
        cost_estimate=cost(4 << 30, 10 * MIB),
        name="forward",
    )(in_hbm(quad_weights), even, in_hbm(field))


def turned_tables(even):
    return pl.pallas_call(
        turned_table_kernel,
        in_specs=[VMEM],
        out_specs=VMEM,
        out_shape=pltpu.HBM((2, 2 * COLS, HALF), bf16),
        compiler_params=params(16),
        cost_estimate=cost(1 << 26, 4 * MIB),
        name="turned_table",
    )(even)


SENT = [jax.ShapeDtypeStruct(PART, f32)] + [jax.ShapeDtypeStruct(PART, bf16)] * 3


def first_analysis(slot_orders, meta, spectra, legendre):
    outs = pl.pallas_call(
        first_analysis_kernel,
        in_specs=[SMEM, SMEM, VMEM, HBM],
        out_specs=[VMEM] * 8,
        out_shape=SENT + [pltpu.VMEM(LOWER, bf16), pltpu.VMEM(UPPER, bf16)] * 2,
        scratch_shapes=[pltpu.VMEM((GROUP, WIDE, M + 128), f32), pltpu.SemaphoreType.DMA((2, PAIRS))],
        compiler_params=params(16),
        cost_estimate=cost(1 << 29, 8 * MIB),
        name="first_analysis",
    )(slot_orders, meta, in_vmem(spectra), in_hbm(legendre))
    return outs[:4], outs[4:6], outs[6:]


def second_analysis(slot_orders, meta, spectra, tables):
    return pl.pallas_call(
        second_analysis_kernel,
        in_specs=[SMEM, SMEM, VMEM, VMEM, VMEM],
        out_specs=[VMEM] * 4,
        out_shape=SENT,
        scratch_shapes=[pltpu.VMEM((GROUP, WIDE, M + 128), f32)],
        compiler_params=params(16),
        cost_estimate=cost(1 << 29, 4 * MIB),
        name="second_analysis",
    )(slot_orders, meta, in_vmem(spectra), *map(in_vmem, tables))


def respond(chunk, slot_orders, meta, response, own, arrived):
    return pl.pallas_call(
        functools.partial(respond_kernel, chunk),
        in_specs=[SMEM, SMEM] + [VMEM] * 5,
        out_specs=VMEM,
        out_shape=jax.ShapeDtypeStruct(PART, bf16),
        compiler_params=params(16),
        cost_estimate=cost(1 << 22, 2 * MIB),
        name="respond",
    )(slot_orders, meta, response, own, *arrived)


def synthesis(chunk, slot_orders, meta, coeffs, tables, earlier):
    return pl.pallas_call(
        functools.partial(synthesis_kernel, chunk),
        in_specs=[SMEM, SMEM] + [VMEM] * 6 + [HBM] * len(earlier),
        out_specs=HBM,
        out_shape=pltpu.HBM(SPECTRA, bf16),
        scratch_shapes=[
            pltpu.VMEM((GROUP, OWNERS, 2, ROWS, WIDE), bf16),
            pltpu.VMEM((GROUP, WIDE, M + 128), f32),
            pltpu.SemaphoreType.DMA((GROUP,)),
        ],
        input_output_aliases={8: 0} if earlier else {},
        compiler_params=params(16),
        cost_estimate=cost(1 << 29, 4 * MIB),
        name="synthesis",
    )(slot_orders, meta, *coeffs, *map(in_vmem, tables), *earlier)


def inverse(synthesized, table):
    return pl.pallas_call(
        inverse_kernel,
        in_specs=[VMEM, HBM],
        out_specs=HBM,
        out_shape=pltpu.HBM((2 * F, ROWS, NLON), bf16),
        scratch_shapes=[
            pltpu.VMEM((2, 2 * COLS, HALF), bf16),
            pltpu.VMEM((2, 2, ROWS, 128, WIDE), f32),
            pltpu.VMEM((2, 2, ROWS, 128, 128), f32),
            pltpu.VMEM((2, F, 2, ROWS, 2 * COLS), bf16),
            pltpu.VMEM((1024, HALF), f32),
            pltpu.VMEM((2, 2, 2 * F, ROWS, TILE), bf16),
            pltpu.SemaphoreType.DMA((TILES,)),
            pltpu.SemaphoreType.DMA((2, 2, 2)),
        ],
        compiler_params=params(36),
        cost_estimate=cost(4 << 30, 14 * MIB),
        name="inverse",
    )(in_vmem(synthesized), in_hbm(table))


def shards(ground_field, legendre, quad_weights, slot_orders, q_response):
    meta = jnp.stack([lax.axis_index("lat"), lax.axis_index("ord")]).astype(jnp.int32)
    first = slot_orders.reshape(COLS, 2)[:, 0]
    even = jnp.where((first & 1) == 0, first, M - 1 - first)
    response = jnp.transpose(q_response, (1, 0, 2))

    spectra = forward(quad_weights, even.reshape(1, COLS), ground_field.reshape(2 * F, ROWS, NLON))
    spectra = swap_owners(spectra)
    sums0, *tables = first_analysis(slot_orders, meta, spectra, legendre)
    sums1 = second_analysis(slot_orders, meta, spectra, tables[1])
    owns = [sums0[0], sums1[0]]
    partials = [exchange(sums0[1:]), exchange(sums1[1:])]
    coeffs = []
    for c in range(CHUNKS):
        induced = respond(c, slot_orders, meta, response, owns[c], partials[c])
        behind1, behind2, behind3 = exchange([induced] * 3)
        coeffs.append((induced, behind3, behind2, behind1))
    synthesized = []
    for c in range(CHUNKS):
        synthesized = [synthesis(c, slot_orders, meta, coeffs[c], tables[c], synthesized)]
    even, synthesized = lax.optimization_barrier((even, synthesized[0]))
    field = inverse(swap_owners(synthesized), turned_tables(even.reshape(COLS, 1)))
    return field.reshape(F, 2, ROWS, NLON)


def solution(mesh):
    in_specs = (
        P(None, None, ("lat", "ord"), None),
        P("ord", "lat", None),
        P(("lat", "ord")),
        P(),
        P(),
    )
    out_specs = P(None, None, ("lat", "ord"), None)
    return jax.shard_map(shards, mesh=mesh, in_specs=in_specs, out_specs=out_specs, check_vma=False)
```
